256 devices in a mesh: section: 2 (over core), seq: 16 (over y, z_hi), head: 8 (over z_lo, x).
Axes of the slice: x: 4, y: 4, z: 8 (z_hi: 4, z_lo: 2; z = z_hi * 2 + z_lo), core: 2. Of those that a mesh axis runs over, the one named last changes fastest.
Arguments:
- queries: bfloat16 [2, 4096, 8192], P('section', 'seq', 'head'), may hold values from -40 to 40
- fresh_kv: bfloat16 [2, 4096, 2048], P('section', 'seq', 'head'), may hold values from -40 to 40
- positions: int32 [4096], replicated, may hold values from 0 to 4095, each once
- cache_kv: bfloat16 [2048, 32, 2048], P('seq', None, 'head'), may hold values from -40 to 40
- cache_lengths: int32 [2048], P('seq'), may hold values from 1 to 32
- out_weight: bfloat16 [8192, 4096], P('head'), may hold values from -0.5 to 0.5
Outputs:
- layer_out: bfloat16 [2, 4096, 4096], P('section', ('seq', 'head'))
The draws below stay inside these ranges and needn't reach their ends.
Inputs may be any that keep to these rules, and one draw needn't show every extreme that they name: `positions`: each of 0 to 4095 appears once.
All inputs are finite; a program needn't handle non-finite values.
Results may differ from the reference program's by a relative error of at most 0.02.
Values may be sent and summed in bfloat16 or wider, within the bound.
No kernel may reach another device: no remote copies, remote signals or barrier semaphores. Data moves between devices by JAX's collectives and lax.ppermute only.
A program may use at most 64 MiB of HBM per device.

```python
import math
import jax
import jax.numpy as jnp
from jax import lax

HQ = 64
KVH = 8
DH = 128
D_WIN = 4096
STEPS = 2
CACHE = 32
SPAN = 4096
REQUESTS = 2048
N_HEAD = 8


def lifted_rows(key, leading):
    noise_key = jax.random.fold_in(key, 0)
    spread_key = jax.random.fold_in(key, 2)
    entries = jax.random.normal(noise_key, leading + (KVH, 2, DH), dtype=jnp.float32)
    spread = jax.random.uniform(spread_key, leading + (KVH, 1), minval=1.0, maxval=1.0)
    key_part = entries[..., 0, :]
    value_part = entries[..., 1, :] * spread
    return jnp.clip(jnp.stack([key_part, value_part], axis=-2), -40.0, 40.0)


def draw_queries(key, part):
    key = jax.random.fold_in(key, 1)
    noise_key = jax.random.fold_in(key, 0)
    entries = jax.random.normal(noise_key, (2, SPAN, KVH, HQ // KVH, DH), dtype=jnp.float32)
    return jnp.clip(entries, -40.0, 40.0).reshape(2, SPAN, HQ * DH).astype(jnp.bfloat16)


def draw_fresh_kv(key, part):
    key = jax.random.fold_in(key, 2)
    entries = lifted_rows(key, (2, SPAN))
    return entries.reshape(2, SPAN, KVH * 2 * DH).astype(jnp.bfloat16)


def draw_cache_kv(key, part):
    key = jax.random.fold_in(key, 3)
    entries = lifted_rows(key, (REQUESTS, CACHE))
    return entries.reshape(REQUESTS, CACHE, KVH * 2 * DH).astype(jnp.bfloat16)


def draw_cache_lengths(key, part):
    key = jax.random.fold_in(key, 4)
    length_key, pick_key = jax.random.split(key)
    lengths = jax.random.randint(length_key, (REQUESTS,), 1, CACHE + 1)
    chosen = jax.random.randint(pick_key, (), 0, REQUESTS)
    return jnp.where(jnp.arange(REQUESTS) == chosen, CACHE, lengths).astype(jnp.int32)


def block_levels(key, shape, cuts, least, largest):
    factor_of, own = 1.0, jax.random.fold_in(key, 6)
    for dim, parts in cuts:
        heights = jnp.exp(jax.random.uniform(jax.random.fold_in(own, dim), (parts,), jnp.float32, least / len(cuts), largest / len(cuts)))
        factor_of = factor_of * jnp.repeat(heights, shape[dim] // parts).reshape([-1 if axis == dim else 1 for axis in range(len(shape))])
    return factor_of


def noise(own_key, shape, scale, limit, shards=(), kind=jnp.bfloat16):
    gain = block_levels(own_key, shape, shards, -0.22, 0.18) if shards else 1.0
    result = jax.random.normal(own_key, shape, jnp.float32) * scale * gain
    return jnp.minimum(jnp.maximum(result, -limit), limit).astype(kind)


def setup_inputs(seed: int = 0) -> dict:
    keys = jax.random.split(jax.random.key(seed), 7)
    return {
        "queries": draw_queries(jax.random.fold_in(keys[6], 71), 0),
        "fresh_kv": draw_fresh_kv(jax.random.fold_in(keys[6], 71), 0),
        "positions": jax.random.permutation(keys[2], SPAN).astype(jnp.int32),
        "cache_kv": draw_cache_kv(jax.random.fold_in(keys[6], 71), 0),
        "cache_lengths": draw_cache_lengths(jax.random.fold_in(keys[6], 71), 0),
        "out_weight": noise(keys[5], (HQ * DH, D_WIN), (HQ * DH // 64) ** -0.5, 0.5, ((0, 8),)),
    }


def rounded(values):
    return lax.optimization_barrier(values.astype(jnp.bfloat16)).astype(jnp.float32)


def reference(queries, fresh_kv, positions, cache_kv, cache_lengths, out_weight):
    groups = HQ // KVH
    score_scale = DH ** -0.5
    prompt_queries = queries[0].astype(jnp.float32).reshape(SPAN, KVH, groups, DH)
    prompt_kv = fresh_kv[0].astype(jnp.float32).reshape(SPAN, KVH, 2, DH)
    prompt_keys = prompt_kv[:, :, 0, :]
    prompt_values = prompt_kv[:, :, 1, :]
    block_rows = math.gcd(SPAN, 64)

    def prompt_block(block_index):
        first_row = block_index * block_rows
        block_queries = lax.dynamic_slice_in_dim(prompt_queries, first_row, block_rows, 0)
        query_pos = lax.dynamic_slice_in_dim(positions, first_row, block_rows, 0)
        scores = jnp.einsum("rhgd,khd->rhgk", block_queries, prompt_keys) * score_scale
        visible = (positions[None, :] <= query_pos[:, None])[:, None, None, :]
        row_max = jnp.max(jnp.where(visible, scores, -jnp.inf), axis=-1, keepdims=True)
        weights = jnp.where(visible, jnp.exp(scores - row_max), 0.0)
        denominator = jnp.sum(weights, axis=-1)
        context = jnp.einsum("rhgk,khd->rhgd", rounded(weights), prompt_values) / denominator[..., None]
        return context.astype(jnp.bfloat16).reshape(block_rows, HQ * DH)

    prompt_out = lax.map(prompt_block, jnp.arange(SPAN // block_rows, dtype=jnp.int32)).reshape(SPAN, HQ * DH)

    sample_queries = queries[1].astype(jnp.float32).reshape(REQUESTS, STEPS, KVH, groups, DH)
    sample_kv = fresh_kv[1].astype(jnp.float32).reshape(REQUESTS, STEPS, KVH, 2, DH)
    cache_all = cache_kv.astype(jnp.float32).reshape(REQUESTS, CACHE, KVH, 2, DH)
    request_block = math.gcd(REQUESTS, 16)
    step_ids = jnp.arange(STEPS, dtype=jnp.int32)
    cache_ids = jnp.arange(CACHE, dtype=jnp.int32)

    def sample_block(block_index):
        first_row = block_index * request_block
        block_queries = lax.dynamic_slice_in_dim(sample_queries, first_row, request_block, 0)
        new_kv = lax.dynamic_slice_in_dim(sample_kv, first_row, request_block, 0)
        own_cache = lax.dynamic_slice_in_dim(cache_all, first_row, request_block, 0)
        own_lengths = lax.dynamic_slice_in_dim(cache_lengths, first_row, request_block, 0)
        prefix_scores = jnp.einsum("rthgd,khd->rthgk", block_queries, prompt_keys) * score_scale
        cache_scores = jnp.einsum("rthgd,rchd->rthgc", block_queries, own_cache[:, :, :, 0, :]) * score_scale
        fresh_scores = jnp.einsum("rthgd,ruhd->rthgu", block_queries, new_kv[:, :, :, 0, :]) * score_scale
        cache_seen = (cache_ids[None, :] < own_lengths[:, None])[:, None, None, None, :]
        fresh_seen = (step_ids[None, :] <= step_ids[:, None])[None, :, None, None, :]
        row_max = jnp.maximum(jnp.max(prefix_scores, axis=-1),
                              jnp.maximum(jnp.max(jnp.where(cache_seen, cache_scores, -jnp.inf), axis=-1),
                                          jnp.max(jnp.where(fresh_seen, fresh_scores, -jnp.inf), axis=-1)))[..., None]
        prefix_weights = jnp.exp(prefix_scores - row_max)
        cache_weights = jnp.where(cache_seen, jnp.exp(cache_scores - row_max), 0.0)
        fresh_weights = jnp.where(fresh_seen, jnp.exp(fresh_scores - row_max), 0.0)
        denominator = jnp.sum(prefix_weights, axis=-1) + jnp.sum(cache_weights, axis=-1) + jnp.sum(fresh_weights, axis=-1)
        context = jnp.einsum("rthgk,khd->rthgd", rounded(prefix_weights), prompt_values)
        context = context + jnp.einsum("rthgc,rchd->rthgd", rounded(cache_weights), own_cache[:, :, :, 1, :])
        context = context + jnp.einsum("rthgu,ruhd->rthgd", rounded(fresh_weights), new_kv[:, :, :, 1, :])
        context = context / denominator[..., None]
        return context.astype(jnp.bfloat16).reshape(request_block * STEPS, HQ * DH)

    sample_out = lax.map(sample_block, jnp.arange(REQUESTS // request_block, dtype=jnp.int32)).reshape(SPAN, HQ * DH)
    flat_rows = jnp.concatenate([prompt_out, sample_out], axis=0)
    group_cols = HQ * DH // N_HEAD
    summed = jnp.zeros((2 * SPAN, D_WIN), jnp.float32)
    for head_group in range(N_HEAD):
        group_term = jnp.dot(flat_rows[:, head_group * group_cols:(head_group + 1) * group_cols],
                             out_weight[head_group * group_cols:(head_group + 1) * group_cols, :],
                             preferred_element_type=jnp.float32)
        summed = summed + rounded(group_term)
    return summed.astype(jnp.bfloat16).reshape(2, SPAN, D_WIN)
```

```python
import functools
import math

import jax
import jax.numpy as jnp
from jax import lax
from jax.experimental import pallas as pl
from jax.experimental.pallas import tpu as pltpu
from jax.sharding import PartitionSpec as P

HQ = 64
KVH = 8
DH = 128
STEPS = 2
CACHE = 32
GROUPS = HQ // KVH
ROWS = 256
HALF = 128
TILE = 32
LHS = TILE * GROUPS
NEG = -1e30
BIG = float(2**22)
EXP_SCALE = DH**-0.5 * math.log2(math.e)
BF16 = jnp.bfloat16
F32 = jnp.float32
VMEM_LIMIT = 56 * 2**20
Z_ORDER = (0, 2, 1, 3)


def seq_perm(dy, dz):
    return [
        (y * 4 + z, ((y + dy) % 4) * 4 + (z + dz) % 4)
        for y in range(4)
        for z in range(4)
    ]


def head_perm(dz, dx):
    return [
        (z * 4 + x, (z ^ dz) * 4 + (x + dx) % 4)
        for z in range(2)
        for x in range(4)
    ]


SWAP = [(0, 1), (1, 0)]
SIDES = ((1, 0), (3, 0), (1, 1), (3, 1))
ACROSS = ((2, 0), (2, 1))


def stacked_queries(q_ref, first_row, first_col):
    stack = jnp.concatenate(
        [q_ref[pl.ds(first_row, TILE), g * DH : (g + 1) * DH] for g in range(GROUPS)],
        axis=0,
    )
    rows = lax.broadcasted_iota(jnp.int32, (LHS, HALF), 0)
    cols = lax.broadcasted_iota(jnp.int32, (LHS, HALF), 1)
    marks = jnp.where((rows & (TILE - 1)) + first_col == cols, -BIG, 0.0).astype(BF16)
    return jnp.concatenate([stack, marks], axis=1)


def column_of(row):
    rows = lax.broadcasted_iota(jnp.int32, (HALF, HALF), 0)
    cols = lax.broadcasted_iota(jnp.int32, (HALF, HALF), 1)
    spread = jnp.where(rows == cols, jnp.broadcast_to(row, (HALF, HALF)), 0.0)
    return jnp.sum(spread, axis=1, keepdims=True)


def absorb(scores, old_max, values):
    width = scores.shape[1]
    top = scores[:, :DH]
    for j in range(DH, width, DH):
        top = jnp.maximum(top, scores[:, j : j + DH])
    new_max = jnp.max(top, axis=1, keepdims=True)
    if old_max is not None:
        new_max = jnp.maximum(old_max, new_max)
    else:
        new_max = jnp.broadcast_to(new_max, (LHS, DH))
    wide = jnp.concatenate([new_max] * (width // DH), axis=1)
    weights = jnp.exp2((scores - wide) * EXP_SCALE).astype(BF16)
    return new_max, jnp.dot(weights, values, preferred_element_type=F32)


def own_kernel(meta, len_ref, q_ref, cache_ref, fresh_ref, m_out, a_out, kt, vs):
    keys = TILE // STEPS * CACHE

    @pl.when(meta[0] == 0)
    def _():
        m_out[...] = jnp.full(m_out.shape, NEG, F32)
        a_out[...] = jnp.zeros(a_out.shape, F32)

    @pl.when(meta[0] == 1)
    def _():
        lengths = column_of(len_ref[0])
        row = lax.broadcasted_iota(jnp.int32, (TILE, keys), 0)
        key = lax.broadcasted_iota(jnp.int32, (TILE, keys), 1)
        same = (key // CACHE) == (row // STEPS)
        nth = (key % CACHE).astype(F32)
        frow = lax.broadcasted_iota(jnp.int32, (TILE, HALF), 0)
        fkey = lax.broadcasted_iota(jnp.int32, (TILE, HALF), 1)
        for t in range(HALF // TILE):
            slot = t % 2
            kt[slot, DH + TILE :, :] = jnp.zeros((DH - TILE, keys + HALF), BF16)
            kt[slot, :DH, :keys] = cache_ref[t * keys : (t + 1) * keys, :DH].T
            kt[slot, :DH, keys:] = fresh_ref[:, :DH].T
            seen = same & (nth < lengths[t * TILE : (t + 1) * TILE])
            kt[slot, DH : DH + TILE, :keys] = jnp.where(seen, 0.0, 1.0).astype(BF16)
            mine = frow + t * TILE
            seen = ((mine // STEPS) == (fkey // STEPS)) & (fkey <= mine)
            kt[slot, DH : DH + TILE, keys:] = jnp.where(seen, 0.0, 1.0).astype(BF16)
            vs[slot, :keys, :DH] = cache_ref[t * keys : (t + 1) * keys, DH:]
            vs[slot, keys:, :DH] = fresh_ref[:, DH:]
            vs[slot, :, DH:] = jnp.ones((keys + HALF, DH), BF16)
            lhs = stacked_queries(q_ref, t * TILE, 0)
            scores = jnp.dot(lhs, kt[slot], preferred_element_type=F32)
            new_max, total = absorb(scores, None, vs[slot])
            m_out[t * LHS : (t + 1) * LHS, :] = new_max
            a_out[t * LHS : (t + 1) * LHS, :] = total


def load_keys(parts, kt, vs, first):
    count = parts[0].shape[0]

    @pl.when(first)
    def _():
        for i, part in enumerate(parts):
            kt[:DH, i * count : (i + 1) * count] = part[:, :DH].T
            vs[i * count : (i + 1) * count, :DH] = part[:, DH:]
        vs[:, DH:] = jnp.ones((len(parts) * count, DH), BF16)


def load_mask(meta, plan, block, pos_ref, kt):
    own = (meta[1] * 4 + meta[2]) * 2
    bound = jnp.where(meta[0] == 1, 1e9, column_of(pos_ref[own + block]))
    pieces = [(dy, dz, flip) for dy, flip in plan for dz in Z_ORDER]
    for j, (dy, dz, flip) in enumerate(pieces):
        source = ((meta[1] - dy) & 3) * 4 + ((meta[2] - dz) & 3)
        key_pos = pos_ref[source * 2 + (meta[0] ^ flip)]
        hidden = jnp.where(key_pos > bound, 1.0, 0.0).astype(BF16)
        kt[DH:, j * HALF : (j + 1) * HALF] = hidden


def prefix_kernel(n_parts, plan, meta, pos_ref, q_ref, *refs):
    parts = refs[:n_parts]
    m_in, a_in, m_out, a_out, kt, vs = refs[n_parts:]
    block = pl.program_id(0)
    load_keys(parts, kt, vs, block == 0)
    load_mask(meta, plan, block, pos_ref, kt)
    tiles = HALF // TILE

    def scores_of(t):
        lhs = stacked_queries(q_ref, t * TILE, t * TILE)
        return jnp.dot(lhs, kt[...], preferred_element_type=F32)

    ready = scores_of(0)
    for t in range(tiles):
        following = scores_of(t + 1) if t + 1 < tiles else None
        rows = slice(t * LHS, (t + 1) * LHS)
        old_max = m_in[rows, :]
        new_max, total = absorb(ready, old_max, vs[...])
        factor = jnp.exp2((old_max - new_max) * EXP_SCALE)
        m_out[rows, :] = new_max
        a_out[rows, :] = a_in[rows, :] * jnp.concatenate([factor, factor], axis=1) + total
        ready = following


W_CHUNKS = 8


def last_kernel(n_parts, plan, meta, pos_ref, q_ref, *refs):
    parts = refs[:n_parts]
    m_in, a_in, w_hbm = refs[n_parts : n_parts + 3]
    outs = refs[n_parts + 3 : n_parts + 7]
    kt, vs, att, w_vmem, sems = refs[n_parts + 7 :]
    cols = w_hbm.shape[1] // W_CHUNKS

    def w_copy(c):
        window = (slice(None), pl.ds(c * cols, cols))
        return pltpu.make_async_copy(w_hbm.at[window], w_vmem.at[window], sems.at[c])

    for c in range(W_CHUNKS):
        w_copy(c).start()
    load_keys(parts, kt, vs, True)
    load_mask(meta, plan, meta[3], pos_ref, kt)
    tiles = HALF // TILE

    def place_of(t):
        return (meta[4] + t) & (tiles - 1)

    def scores_of(t):
        start = pl.multiple_of(place_of(t) * TILE, TILE)
        lhs = stacked_queries(q_ref, start, start)
        return jnp.dot(lhs, kt[...], preferred_element_type=F32)

    ready = scores_of(0)
    for t in range(tiles):
        following = scores_of(t + 1) if t + 1 < tiles else None
        rows = pl.ds(pl.multiple_of(place_of(t) * LHS, LHS), LHS)
        old_max = m_in[rows, :]
        new_max, total = absorb(ready, old_max, vs[...])
        factor = jnp.exp2((old_max - new_max) * EXP_SCALE)
        total = a_in[rows, :] * jnp.concatenate([factor, factor], axis=1) + total
        attended = (total[:, :DH] / total[:, DH:]).astype(BF16)
        for g in range(GROUPS):
            att[t * TILE : (t + 1) * TILE, g * DH : (g + 1) * DH] = attended[
                g * TILE : (g + 1) * TILE
            ]
        ready = following
    for c in range(W_CHUNKS):
        w_copy(c).wait()
        window = slice(c * cols, (c + 1) * cols)
        term = jnp.dot(att[...], w_vmem[:, window], preferred_element_type=F32).astype(BF16)
        for t in range(tiles):
            outs[t][:, window] = term[t * TILE : (t + 1) * TILE]


def params():
    return pltpu.CompilerParams(
        vmem_limit_bytes=VMEM_LIMIT, dimension_semantics=("arbitrary",)
    )


def cost(keys, rows=ROWS, extra=0):
    work = rows * GROUPS * keys
    return pl.CostEstimate(
        flops=8 * DH * work + extra, bytes_accessed=6 * 2**20, transcendentals=work
    )


def whole(shape):
    return pl.BlockSpec(shape, lambda i, meta: (0,) * len(shape))


def own_call(meta, lengths, q, cache, fresh):
    keys = TILE // STEPS * CACHE + HALF
    cache_rows = HALF // STEPS * CACHE
    return pl.pallas_call(
        own_kernel,
        grid_spec=pltpu.PrefetchScalarGridSpec(
            num_scalar_prefetch=1,
            grid=(ROWS // HALF,),
            in_specs=[
                pl.BlockSpec((1, 1, HALF), lambda i, meta: (i, 0, 0)),
                pl.BlockSpec((HALF, GROUPS * DH), lambda i, meta: (i, 0)),
                pl.BlockSpec((cache_rows, 2 * DH), lambda i, meta: (i, 0)),
                pl.BlockSpec((HALF, 2 * DH), lambda i, meta: (i, 0)),
            ],
            out_specs=[
                pl.BlockSpec((HALF * GROUPS, DH), lambda i, meta: (i, 0)),
                pl.BlockSpec((HALF * GROUPS, 2 * DH), lambda i, meta: (i, 0)),
            ],
            scratch_shapes=[
                pltpu.VMEM((2, 2 * DH, keys), BF16),
                pltpu.VMEM((2, keys, 2 * DH), BF16),
            ],
        ),
        out_shape=[
            jax.ShapeDtypeStruct((ROWS * GROUPS, DH), F32),
            jax.ShapeDtypeStruct((ROWS * GROUPS, 2 * DH), F32),
        ],
        compiler_params=params(),
        cost_estimate=cost(keys),
        name="own_keys",
    )(meta, lengths, q, cache, fresh)


def prefix_call(name, plan, meta, pos, q, parts, state):
    n_parts = len(parts)
    keys = sum(p.shape[0] for p in parts)
    state_specs = [
        pl.BlockSpec((HALF * GROUPS, DH), lambda i, meta: (i, 0)),
        pl.BlockSpec((HALF * GROUPS, 2 * DH), lambda i, meta: (i, 0)),
    ]
    return pl.pallas_call(
        functools.partial(prefix_kernel, n_parts, plan),
        grid_spec=pltpu.PrefetchScalarGridSpec(
            num_scalar_prefetch=1,
            grid=(ROWS // HALF,),
            in_specs=[
                whole(pos.shape),
                pl.BlockSpec((HALF, GROUPS * DH), lambda i, meta: (i, 0)),
            ]
            + [whole(p.shape) for p in parts]
            + state_specs,
            out_specs=state_specs,
            scratch_shapes=[
                pltpu.VMEM((2 * DH, keys), BF16),
                pltpu.VMEM((keys, 2 * DH), BF16),
            ],
        ),
        out_shape=[jax.ShapeDtypeStruct(s.shape, F32) for s in state],
        input_output_aliases={3 + n_parts: 0, 4 + n_parts: 1},
        compiler_params=params(),
        cost_estimate=cost(keys),
        name=name,
    )(meta, pos, q, *parts, *state)


def last_call(name, plan, meta, pos, q, parts, state, out_weight):
    n_parts = len(parts)
    keys = sum(p.shape[0] for p in parts)
    width = out_weight.shape[1]
    tiles = HALF // TILE
    return pl.pallas_call(
        functools.partial(last_kernel, n_parts, plan),
        grid_spec=pltpu.PrefetchScalarGridSpec(
            num_scalar_prefetch=1,
            grid=(1,),
            in_specs=[
                whole(pos.shape),
                pl.BlockSpec((HALF, GROUPS * DH), lambda i, meta: (meta[3], 0)),
            ]
            + [whole(p.shape) for p in parts]
            + [
                pl.BlockSpec((HALF * GROUPS, DH), lambda i, meta: (meta[3], 0)),
                pl.BlockSpec((HALF * GROUPS, 2 * DH), lambda i, meta: (meta[3], 0)),
                pl.BlockSpec(memory_space=pl.ANY),
            ],
            out_specs=[whole((TILE, width))] * tiles,
            scratch_shapes=[
                pltpu.VMEM((2 * DH, keys), BF16),
                pltpu.VMEM((keys, 2 * DH), BF16),
                pltpu.VMEM((HALF, GROUPS * DH), BF16),
                pltpu.VMEM(out_weight.shape, BF16),
                pltpu.SemaphoreType.DMA((W_CHUNKS,)),
            ],
        ),
        out_shape=[jax.ShapeDtypeStruct((TILE, width), BF16)] * tiles,
        compiler_params=params(),
        cost_estimate=cost(keys, HALF, 2 * HALF * out_weight.size),
        name=name,
    )(meta, pos, q, *parts, *state, out_weight)


def on_device(queries, fresh_kv, positions, cache_kv, cache_lengths, out_weight):
    q = queries[0]
    own_kv = fresh_kv[0]
    section = lax.axis_index("section")
    seq = lax.axis_index("seq")
    head = lax.axis_index("head")

    other_half = lax.ppermute(own_kv[HALF:], "section", SWAP)
    mine = jnp.where(section == 0, own_kv[:HALF], other_half)
    near = jnp.concatenate(
        [mine] + [lax.ppermute(mine, "seq", seq_perm(0, d)) for d in Z_ORDER[1:]], axis=0
    )
    far = {d: lax.ppermute(near, "seq", seq_perm(d, 0)) for d in (2, 1, 3)}
    far[0] = near
    swapped = {d: lax.ppermute(far[d], "section", SWAP) for d in (0, 1, 3, 2)}

    def meta_of(block):
        return jnp.stack([section, seq >> 2, seq & 3, block, head & 3])

    head_z = head >> 2
    meta_a, meta_b = meta_of(1 - head_z), meta_of(head_z)
    pos = positions.astype(F32).reshape(2 * 16, 1, HALF)
    lengths = jnp.repeat(cache_lengths, STEPS).astype(F32).reshape(2, 1, HALF)
    cache = cache_kv.reshape(ROWS // STEPS * CACHE, 2 * DH)

    state = own_call(meta_a, lengths, q, cache, own_kv)
    state = prefix_call("near_keys", ((0, 0), (0, 1)), meta_a, pos, q, [far[0], swapped[0]], state)
    state = prefix_call(
        "side_keys", SIDES, meta_a, pos, q, [far[1], far[3], swapped[1], swapped[3]], state
    )
    across = [far[2], swapped[2]]
    terms_a = last_call("across_keys_a", ACROSS, meta_a, pos, q, across, state, out_weight)
    got = [
        lax.ppermute(terms_a[dx], "head", head_perm(1, dx)) for dx in (2, 1, 3, 0)
    ]
    terms_b = last_call("across_keys_b", ACROSS, meta_b, pos, q, across, state, out_weight)
    got += [lax.ppermute(terms_b[dx], "head", head_perm(0, dx)) for dx in (2, 1, 3)]
    summed = terms_b[0].astype(F32)
    for term in got:
        summed = summed + term.astype(F32)
    return summed.astype(BF16)[None]


def solution(mesh):
    in_specs = (
        P("section", "seq", "head"),
        P("section", "seq", "head"),
        P(),
        P("seq", None, "head"),
        P("seq"),
        P("head", None),
    )
    out_specs = P("section", ("seq", "head"), None)
    return jax.shard_map(
        on_device, mesh=mesh, in_specs=in_specs, out_specs=out_specs, check_vma=False
    )
```

```python
import functools
import math

import jax
import jax.numpy as jnp
from jax import lax
from jax.experimental import pallas as pl
from jax.experimental.pallas import tpu as pltpu
from jax.sharding import PartitionSpec as P

HQ = 64
KVH = 8
DH = 128
STEPS = 2
CACHE = 32
GROUPS = HQ // KVH
ROWS = 256
HALF = 128
TILE = 32
LHS = TILE * GROUPS
NEG = -1e30
BIG = float(2**22)
EXP_SCALE = DH**-0.5 * math.log2(math.e)
BF16 = jnp.bfloat16
F32 = jnp.float32
Z_ORDER = (0, 2, 1, 3)


def seq_perm(dy, dz):
    return [
        (y * 4 + z, ((y + dy) % 4) * 4 + (z + dz) % 4)
        for y in range(4)
        for z in range(4)
    ]


def head_perm(dz, dx):
    return [
        (z * 4 + x, (z ^ dz) * 4 + (x + dx) % 4)
        for z in range(2)
        for x in range(4)
    ]


SWAP = [(0, 1), (1, 0)]
FAR = tuple((dy, flip) for flip in (0, 1) for dy in (1, 3, 2))


def stacked_queries(q_ref, first_row, first_col):
    stack = jnp.concatenate(
        [q_ref[pl.ds(first_row, TILE), g * DH : (g + 1) * DH] for g in range(GROUPS)],
        axis=0,
    )
    rows = lax.broadcasted_iota(jnp.int32, (LHS, HALF), 0)
    cols = lax.broadcasted_iota(jnp.int32, (LHS, HALF), 1)
    marks = jnp.where((rows & (TILE - 1)) + first_col == cols, -BIG, 0.0).astype(BF16)
    return jnp.concatenate([stack, marks], axis=1)


def column_of(row):
    rows = lax.broadcasted_iota(jnp.int32, (HALF, HALF), 0)
    cols = lax.broadcasted_iota(jnp.int32, (HALF, HALF), 1)
    spread = jnp.where(rows == cols, jnp.broadcast_to(row, (HALF, HALF)), 0.0)
    return jnp.sum(spread, axis=1, keepdims=True)


def absorb(scores, old_max, values):
    width = scores.shape[1]
    top = scores[:, :DH]
    for j in range(DH, width, DH):
        top = jnp.maximum(top, scores[:, j : j + DH])
    new_max = jnp.max(top, axis=1, keepdims=True)
    if old_max is not None:
        new_max = jnp.maximum(old_max, new_max)
    else:
        new_max = jnp.broadcast_to(new_max, (LHS, DH))
    wide = jnp.concatenate([new_max] * (width // DH), axis=1)
    weights = jnp.exp2((scores - wide) * EXP_SCALE).astype(BF16)
    return new_max, jnp.dot(weights, values, preferred_element_type=F32)


def own_kernel(meta, len_ref, q_ref, cache_ref, fresh_ref, m_out, a_out, kt, vs):
    keys = TILE // STEPS * CACHE

    @pl.when(meta[0] == 0)
    def _():
        m_out[...] = jnp.full(m_out.shape, NEG, F32)
        a_out[...] = jnp.zeros(a_out.shape, F32)

    @pl.when(meta[0] == 1)
    def _():
        lengths = column_of(len_ref[0])
        row = lax.broadcasted_iota(jnp.int32, (TILE, keys), 0)
        key = lax.broadcasted_iota(jnp.int32, (TILE, keys), 1)
        same = (key // CACHE) == (row // STEPS)
        nth = (key % CACHE).astype(F32)
        frow = lax.broadcasted_iota(jnp.int32, (TILE, HALF), 0)
        fkey = lax.broadcasted_iota(jnp.int32, (TILE, HALF), 1)
        for t in range(HALF // TILE):
            slot = t % 2
            kt[slot, DH + TILE :, :] = jnp.zeros((DH - TILE, keys + HALF), BF16)
            kt[slot, :DH, :keys] = cache_ref[t * keys : (t + 1) * keys, :DH].T
            kt[slot, :DH, keys:] = fresh_ref[:, :DH].T
            seen = same & (nth < lengths[t * TILE : (t + 1) * TILE])
            kt[slot, DH : DH + TILE, :keys] = jnp.where(seen, 0.0, 1.0).astype(BF16)
            mine = frow + t * TILE
            seen = ((mine // STEPS) == (fkey // STEPS)) & (fkey <= mine)
            kt[slot, DH : DH + TILE, keys:] = jnp.where(seen, 0.0, 1.0).astype(BF16)
            vs[slot, :keys, :DH] = cache_ref[t * keys : (t + 1) * keys, DH:]
            vs[slot, keys:, :DH] = fresh_ref[:, DH:]
            vs[slot, :, DH:] = jnp.ones((keys + HALF, DH), BF16)
            lhs = stacked_queries(q_ref, t * TILE, 0)
            scores = jnp.dot(lhs, kt[slot], preferred_element_type=F32)
            new_max, total = absorb(scores, None, vs[slot])
            m_out[t * LHS : (t + 1) * LHS, :] = new_max
            a_out[t * LHS : (t + 1) * LHS, :] = total


def load_keys(parts, kt, vs, first):
    count = parts[0].shape[0]

    @pl.when(first)
    def _():
        for i, part in enumerate(parts):
            kt[:DH, i * count : (i + 1) * count] = part[:, :DH].T
            vs[i * count : (i + 1) * count, :DH] = part[:, DH:]
        vs[:, DH:] = jnp.ones((len(parts) * count, DH), BF16)


def load_mask(meta, plan, block, pos_ref, kt):
    own = (meta[1] * 4 + meta[2]) * 2
    bound = jnp.where(meta[0] == 1, 1e9, column_of(pos_ref[own + block]))
    pieces = [(dy, dz, flip) for dy, flip in plan for dz in Z_ORDER]
    for j, (dy, dz, flip) in enumerate(pieces):
        source = ((meta[1] - dy) & 3) * 4 + ((meta[2] - dz) & 3)
        key_pos = pos_ref[source * 2 + (meta[0] ^ flip)]
        hidden = jnp.where(key_pos > bound, 1.0, 0.0).astype(BF16)
        kt[DH:, j * HALF : (j + 1) * HALF] = hidden


def prefix_kernel(n_parts, plan, meta, pos_ref, q_ref, *refs):
    parts = refs[:n_parts]
    m_in, a_in, m_out, a_out, kt, vs = refs[n_parts:]
    block = pl.program_id(0)
    load_keys(parts, kt, vs, block == 0)
    load_mask(meta, plan, block, pos_ref, kt)
    tiles = HALF // TILE

    def scores_of(t):
        lhs = stacked_queries(q_ref, t * TILE, t * TILE)
        return jnp.dot(lhs, kt[...], preferred_element_type=F32)

    ready = scores_of(0)
    for t in range(tiles):
        following = scores_of(t + 1) if t + 1 < tiles else None
        rows = slice(t * LHS, (t + 1) * LHS)
        old_max = m_in[rows, :]
        new_max, total = absorb(ready, old_max, vs[...])
        factor = jnp.exp2((old_max - new_max) * EXP_SCALE)
        m_out[rows, :] = new_max
        a_out[rows, :] = a_in[rows, :] * jnp.concatenate([factor, factor], axis=1) + total
        ready = following


W_CHUNKS = 8


def last_kernel(n_parts, plan, meta, pos_ref, q_ref, *refs):
    parts = refs[:n_parts]
    m_in, a_in, w_hbm = refs[n_parts : n_parts + 3]
    ahead, behind, over, beside, beyond, home = refs[n_parts + 3 : n_parts + 9]
    kt, vs, att, w_vmem, sems = refs[n_parts + 9 :]
    cols = w_hbm.shape[1] // W_CHUNKS
    step = pl.program_id(0)

    def w_copy(c):
        window = (slice(None), pl.ds(c * cols, cols))
        return pltpu.make_async_copy(w_hbm.at[window], w_vmem.at[window], sems.at[c])

    @pl.when(step == 0)
    def _():
        for c in range(W_CHUNKS):
            w_copy(c).start()

    load_keys(parts, kt, vs, step == 0)
    load_mask(meta, plan, meta[3] ^ step, pos_ref, kt)
    tiles = HALF // TILE

    def place_of(t):
        return (meta[4] + t) & (tiles - 1)

    def scores_of(t):
        start = pl.multiple_of(place_of(t) * TILE, TILE)
        lhs = stacked_queries(q_ref, start, start)
        return jnp.dot(lhs, kt[...], preferred_element_type=F32)

    ready = scores_of(0)
    for t in range(tiles):
        following = scores_of(t + 1) if t + 1 < tiles else None
        rows = pl.ds(pl.multiple_of(place_of(t) * LHS, LHS), LHS)
        old_max = m_in[rows, :]
        new_max, total = absorb(ready, old_max, vs[...])
        factor = jnp.exp2((old_max - new_max) * EXP_SCALE)
        total = a_in[rows, :] * jnp.concatenate([factor, factor], axis=1) + total
        attended = (total[:, :DH] / total[:, DH:]).astype(BF16)
        first = pl.multiple_of(step * HALF + t * TILE, TILE)
        for g in range(GROUPS):
            att[pl.ds(first, TILE), g * DH : (g + 1) * DH] = attended[
                g * TILE : (g + 1) * TILE
            ]
        ready = following

    @pl.when(step == 1)
    def _():
        for c in range(W_CHUNKS):
            w_copy(c).wait()
            window = slice(c * cols, (c + 1) * cols)
            term = jnp.dot(att[...], w_vmem[:, window], preferred_element_type=F32)
            term = term.astype(BF16)

            def piece(dz, dx):
                first = (1 - dz) * HALF + dx * TILE
                return term[first : first + TILE]

            ahead[:TILE, window] = piece(0, 1)
            ahead[TILE:, window] = piece(1, 1)
            behind[:TILE, window] = piece(0, 3)
            behind[TILE:, window] = piece(1, 3)
            over[:, window] = piece(1, 2)
            beside[:, window] = piece(1, 0)
            beyond[:, window] = piece(0, 2)
            home[:, window] = piece(0, 0)


def params(mebibytes):
    return pltpu.CompilerParams(
        vmem_limit_bytes=mebibytes * 2**20, dimension_semantics=("arbitrary",)
    )


def cost(keys, rows=ROWS, extra=0):
    work = rows * GROUPS * keys
    return pl.CostEstimate(
        flops=8 * DH * work + extra, bytes_accessed=6 * 2**20, transcendentals=work
    )


def whole(shape):
    return pl.BlockSpec(shape, lambda i, meta: (0,) * len(shape))


def own_call(meta, lengths, q, cache, fresh):
    keys = TILE // STEPS * CACHE + HALF
    cache_rows = HALF // STEPS * CACHE
    return pl.pallas_call(
        own_kernel,
        grid_spec=pltpu.PrefetchScalarGridSpec(
            num_scalar_prefetch=1,
            grid=(ROWS // HALF,),
            in_specs=[
                pl.BlockSpec((1, 1, HALF), lambda i, meta: (i, 0, 0)),
                pl.BlockSpec((HALF, GROUPS * DH), lambda i, meta: (i, 0)),
                pl.BlockSpec((cache_rows, 2 * DH), lambda i, meta: (i, 0)),
                pl.BlockSpec((HALF, 2 * DH), lambda i, meta: (i, 0)),
            ],
            out_specs=[
                pl.BlockSpec((HALF * GROUPS, DH), lambda i, meta: (i, 0)),
                pl.BlockSpec((HALF * GROUPS, 2 * DH), lambda i, meta: (i, 0)),
            ],
            scratch_shapes=[
                pltpu.VMEM((2, 2 * DH, keys), BF16),
                pltpu.VMEM((2, keys, 2 * DH), BF16),
            ],
        ),
        out_shape=[
            jax.ShapeDtypeStruct((ROWS * GROUPS, DH), F32),
            jax.ShapeDtypeStruct((ROWS * GROUPS, 2 * DH), F32),
        ],
        compiler_params=params(20),
        cost_estimate=cost(keys),
        name="own_keys",
    )(meta, lengths, q, cache, fresh)


def prefix_call(name, plan, meta, pos, q, parts, state):
    n_parts = len(parts)
    keys = sum(p.shape[0] for p in parts)
    state_specs = [
        pl.BlockSpec((HALF * GROUPS, DH), lambda i, meta: (i, 0)),
        pl.BlockSpec((HALF * GROUPS, 2 * DH), lambda i, meta: (i, 0)),
    ]
    return pl.pallas_call(
        functools.partial(prefix_kernel, n_parts, plan),
        grid_spec=pltpu.PrefetchScalarGridSpec(
            num_scalar_prefetch=1,
            grid=(ROWS // HALF,),
            in_specs=[
                whole(pos.shape),
                pl.BlockSpec((HALF, GROUPS * DH), lambda i, meta: (i, 0)),
            ]
            + [whole(p.shape) for p in parts]
            + state_specs,
            out_specs=state_specs,
            scratch_shapes=[
                pltpu.VMEM((2 * DH, keys), BF16),
                pltpu.VMEM((keys, 2 * DH), BF16),
            ],
        ),
        out_shape=[jax.ShapeDtypeStruct(s.shape, F32) for s in state],
        input_output_aliases={3 + n_parts: 0, 4 + n_parts: 1},
        compiler_params=params(20),
        cost_estimate=cost(keys),
        name=name,
    )(meta, pos, q, *parts, *state)


def last_call(name, plan, meta, pos, q, parts, state, out_weight):
    n_parts = len(parts)
    keys = sum(p.shape[0] for p in parts)
    width = out_weight.shape[1]
    sizes = (2 * TILE, 2 * TILE, TILE, TILE, TILE, TILE)
    return pl.pallas_call(
        functools.partial(last_kernel, n_parts, plan),
        grid_spec=pltpu.PrefetchScalarGridSpec(
            num_scalar_prefetch=1,
            grid=(ROWS // HALF,),
            in_specs=[
                whole(pos.shape),
                pl.BlockSpec((HALF, GROUPS * DH), lambda i, meta: (meta[3] ^ i, 0)),
            ]
            + [whole(p.shape) for p in parts]
            + [
                pl.BlockSpec((HALF * GROUPS, DH), lambda i, meta: (meta[3] ^ i, 0)),
                pl.BlockSpec((HALF * GROUPS, 2 * DH), lambda i, meta: (meta[3] ^ i, 0)),
                pl.BlockSpec(memory_space=pl.ANY),
            ],
            out_specs=[whole((size, width)) for size in sizes],
            scratch_shapes=[
                pltpu.VMEM((2 * DH, keys), BF16),
                pltpu.VMEM((keys, 2 * DH), BF16),
                pltpu.VMEM((ROWS, GROUPS * DH), BF16),
                pltpu.VMEM(out_weight.shape, BF16),
                pltpu.SemaphoreType.DMA((W_CHUNKS,)),
            ],
        ),
        out_shape=[jax.ShapeDtypeStruct((size, width), BF16) for size in sizes],
        compiler_params=params(36),
        cost_estimate=cost(keys, ROWS, 2 * ROWS * out_weight.size),
        name=name,
    )(meta, pos, q, *parts, *state, out_weight)


def on_device(queries, fresh_kv, positions, cache_kv, cache_lengths, out_weight):
    q = queries[0]
    own_kv = fresh_kv[0]
    section = lax.axis_index("section")
    seq = lax.axis_index("seq")
    head = lax.axis_index("head")

    meta = jnp.stack([section, seq >> 2, seq & 3, 1 - (head >> 2), head & 3])
    pos = positions.astype(F32).reshape(2 * 16, 1, HALF)
    lengths = jnp.repeat(cache_lengths, STEPS).astype(F32).reshape(2, 1, HALF)
    cache = cache_kv.reshape(ROWS // STEPS * CACHE, 2 * DH)

    other_half = lax.ppermute(own_kv[HALF:], "section", SWAP)
    mine = jnp.where(section == 0, own_kv[:HALF], other_half)
    blocks = [mine] + [lax.ppermute(mine, "seq", seq_perm(0, d)) for d in Z_ORDER[1:]]
    own_inputs = lax.optimization_barrier((mine, meta, lengths, pos))
    _, meta, lengths, pos = own_inputs
    state = own_call(meta, lengths, q, cache, own_kv)
    blocks[3], state = lax.optimization_barrier((blocks[3], state))
    near = jnp.concatenate(blocks, axis=0)
    far = {d: lax.ppermute(near, "seq", seq_perm(d, 0)) for d in (1, 3, 2)}
    near_swapped = lax.ppermute(near, "section", SWAP)
    state = prefix_call(
        "near_keys", ((0, 0), (0, 1)), meta, pos, q, [near, near_swapped], state
    )
    far, state = lax.optimization_barrier((far, state))
    swapped = {d: lax.ppermute(far[d], "section", SWAP) for d in (1, 3, 2)}
    parts = [far[d] for d in (1, 3, 2)] + [swapped[d] for d in (1, 3, 2)]
    ahead, behind, over, beside, beyond, home = last_call(
        "far_keys", FAR, meta, pos, q, parts, state, out_weight
    )
    crossed = lax.ppermute(over, "head", head_perm(1, 0))
    from_left = lax.ppermute(ahead, "head", head_perm(0, 1))
    from_right = lax.ppermute(behind, "head", head_perm(0, 3))
    opposite = lax.ppermute(added(crossed, beyond), "head", head_perm(0, 2))
    mirror = added(from_left[TILE:], from_right[TILE:], beside)
    mirror = lax.ppermute(mirror, "head", head_perm(1, 0))
    return added(home, from_left[:TILE], from_right[:TILE], opposite, mirror)[None]


def added(first, *others):
    total = first.astype(F32)
    for other in others:
        total = total + other.astype(F32)
    return total.astype(BF16)


def solution(mesh):
    in_specs = (
        P("section", "seq", "head"),
        P("section", "seq", "head"),
        P(),
        P("seq", None, "head"),
        P("seq"),
        P("head", None),
    )
    out_specs = P("section", ("seq", "head"), None)
    return jax.shard_map(
        on_device, mesh=mesh, in_specs=in_specs, out_specs=out_specs, check_vma=False
    )
```

```python
import functools
import math

import jax
import jax.numpy as jnp
from jax import lax
from jax.experimental import pallas as pl
from jax.experimental.pallas import tpu as pltpu
from jax.sharding import PartitionSpec as P

HQ = 64
KVH = 8
DH = 128
STEPS = 2
CACHE = 32
GROUPS = HQ // KVH
ROWS = 256
HALF = 128
TILE = 32
LHS = TILE * GROUPS
NEG = -1e30
BIG = float(2**22)
EXP_SCALE = DH**-0.5 * math.log2(math.e)
BF16 = jnp.bfloat16
F32 = jnp.float32
Z_ORDER = (0, 2, 1, 3)


def seq_perm(dy, dz):
    return [
        (y * 4 + z, ((y + dy) % 4) * 4 + (z + dz) % 4)
        for y in range(4)
        for z in range(4)
    ]


def head_perm(dz, dx):
    return [
        (z * 4 + x, (z ^ dz) * 4 + (x + dx) % 4)
        for z in range(2)
        for x in range(4)
    ]


SWAP = [(0, 1), (1, 0)]
NEAR = ((0, 0), (0, 1))
SIDES = ((1, 0), (3, 0), (1, 1), (3, 1))
ACROSS = ((2, 0), (2, 1))
PLACES = tuple((dz, dx) for dz in (1, 0) for dx in range(4))


def stacked_queries(q_ref, first_row, first_col):
    stack = jnp.concatenate(
        [q_ref[pl.ds(first_row, TILE), g * DH : (g + 1) * DH] for g in range(GROUPS)],
        axis=0,
    )
    rows = lax.broadcasted_iota(jnp.int32, (LHS, HALF), 0)
    cols = lax.broadcasted_iota(jnp.int32, (LHS, HALF), 1)
    marks = jnp.where((rows & (TILE - 1)) + first_col == cols, -BIG, 0.0).astype(BF16)
    return jnp.concatenate([stack, marks], axis=1)


def column_of(row):
    rows = lax.broadcasted_iota(jnp.int32, (HALF, HALF), 0)
    cols = lax.broadcasted_iota(jnp.int32, (HALF, HALF), 1)
    spread = jnp.where(rows == cols, jnp.broadcast_to(row, (HALF, HALF)), 0.0)
    return jnp.sum(spread, axis=1, keepdims=True)


def absorb(scores, old_max, values):
    width = scores.shape[1]
    top = scores[:, :DH]
    for j in range(DH, width, DH):
        top = jnp.maximum(top, scores[:, j : j + DH])
    new_max = jnp.max(top, axis=1, keepdims=True)
    if old_max is not None:
        new_max = jnp.maximum(old_max, new_max)
    else:
        new_max = jnp.broadcast_to(new_max, (LHS, DH))
    wide = jnp.concatenate([new_max] * (width // DH), axis=1)
    weights = jnp.exp2((scores - wide) * EXP_SCALE).astype(BF16)
    return new_max, jnp.dot(weights, values, preferred_element_type=F32)


def own_kernel(meta, len_ref, q_ref, cache_ref, fresh_ref, m_out, a_out, kt, vs):
    keys = TILE // STEPS * CACHE

    @pl.when(meta[0] == 0)
    def _():
        m_out[...] = jnp.full(m_out.shape, NEG, F32)
        a_out[...] = jnp.zeros(a_out.shape, F32)

    @pl.when(meta[0] == 1)
    def _():
        lengths = column_of(len_ref[0])
        row = lax.broadcasted_iota(jnp.int32, (TILE, keys), 0)
        key = lax.broadcasted_iota(jnp.int32, (TILE, keys), 1)
        same = (key // CACHE) == (row // STEPS)
        nth = (key % CACHE).astype(F32)
        frow = lax.broadcasted_iota(jnp.int32, (TILE, HALF), 0)
        fkey = lax.broadcasted_iota(jnp.int32, (TILE, HALF), 1)
        for t in range(HALF // TILE):
            slot = t % 2
            kt[slot, DH + TILE :, :] = jnp.zeros((DH - TILE, keys + HALF), BF16)
            kt[slot, :DH, :keys] = cache_ref[t * keys : (t + 1) * keys, :DH].T
            kt[slot, :DH, keys:] = fresh_ref[:, :DH].T
            seen = same & (nth < lengths[t * TILE : (t + 1) * TILE])
            kt[slot, DH : DH + TILE, :keys] = jnp.where(seen, 0.0, 1.0).astype(BF16)
            mine = frow + t * TILE
            seen = ((mine // STEPS) == (fkey // STEPS)) & (fkey <= mine)
            kt[slot, DH : DH + TILE, keys:] = jnp.where(seen, 0.0, 1.0).astype(BF16)
            vs[slot, :keys, :DH] = cache_ref[t * keys : (t + 1) * keys, DH:]
            vs[slot, keys:, :DH] = fresh_ref[:, DH:]
            vs[slot, :, DH:] = jnp.ones((keys + HALF, DH), BF16)
            lhs = stacked_queries(q_ref, t * TILE, 0)
            scores = jnp.dot(lhs, kt[slot], preferred_element_type=F32)
            new_max, total = absorb(scores, None, vs[slot])
            m_out[t * LHS : (t + 1) * LHS, :] = new_max
            a_out[t * LHS : (t + 1) * LHS, :] = total


def load_keys(parts, kt, vs, first):
    count = parts[0].shape[0]

    @pl.when(first)
    def _():
        for i, part in enumerate(parts):
            kt[:DH, i * count : (i + 1) * count] = part[:, :DH].T
            vs[i * count : (i + 1) * count, :DH] = part[:, DH:]
        vs[:, DH:] = jnp.ones((len(parts) * count, DH), BF16)


def load_mask(meta, plan, block, pos_ref, kt):
    own = (meta[1] * 4 + meta[2]) * 2
    bound = jnp.where(meta[0] == 1, 1e9, column_of(pos_ref[own + block]))
    pieces = [(dy, dz, flip) for dy, flip in plan for dz in Z_ORDER]
    for j, (dy, dz, flip) in enumerate(pieces):
        source = ((meta[1] - dy) & 3) * 4 + ((meta[2] - dz) & 3)
        key_pos = pos_ref[source * 2 + (meta[0] ^ flip)]
        hidden = jnp.where(key_pos > bound, 1.0, 0.0).astype(BF16)
        kt[DH:, j * HALF : (j + 1) * HALF] = hidden


def prefix_kernel(n_parts, plan, meta, pos_ref, q_ref, *refs):
    parts = refs[:n_parts]
    m_in, a_in, m_out, a_out, kt, vs = refs[n_parts:]
    block = pl.program_id(0)
    load_keys(parts, kt, vs, block == 0)
    load_mask(meta, plan, block, pos_ref, kt)
    tiles = HALF // TILE

    def scores_of(t):
        lhs = stacked_queries(q_ref, t * TILE, t * TILE)
        return jnp.dot(lhs, kt[...], preferred_element_type=F32)

    ready = scores_of(0)
    for t in range(tiles):
        following = scores_of(t + 1) if t + 1 < tiles else None
        rows = slice(t * LHS, (t + 1) * LHS)
        old_max = m_in[rows, :]
        new_max, total = absorb(ready, old_max, vs[...])
        factor = jnp.exp2((old_max - new_max) * EXP_SCALE)
        m_out[rows, :] = new_max
        a_out[rows, :] = a_in[rows, :] * jnp.concatenate([factor, factor], axis=1) + total
        ready = following


W_CHUNKS = 8


def last_kernel(n_parts, plan, meta, pos_ref, q_ref, *refs):
    parts = refs[:n_parts]
    m_in, a_in, w_hbm = refs[n_parts : n_parts + 3]
    outs = refs[n_parts + 3 : n_parts + 11]
    kt, vs, att, w_vmem, sems = refs[n_parts + 11 :]
    cols = w_hbm.shape[1] // W_CHUNKS
    step = pl.program_id(0)

    def w_copy(c):
        window = (slice(None), pl.ds(c * cols, cols))
        return pltpu.make_async_copy(w_hbm.at[window], w_vmem.at[window], sems.at[c])

    @pl.when(step == 0)
    def _():
        for c in range(W_CHUNKS):
            w_copy(c).start()

    load_keys(parts, kt, vs, step == 0)
    load_mask(meta, plan, meta[3] ^ step, pos_ref, kt)
    tiles = HALF // TILE

    def place_of(t):
        return (meta[4] + t) & (tiles - 1)

    def scores_of(t):
        start = pl.multiple_of(place_of(t) * TILE, TILE)
        lhs = stacked_queries(q_ref, start, start)
        return jnp.dot(lhs, kt[...], preferred_element_type=F32)

    ready = scores_of(0)
    for t in range(tiles):
        following = scores_of(t + 1) if t + 1 < tiles else None
        rows = pl.ds(pl.multiple_of(place_of(t) * LHS, LHS), LHS)
        old_max = m_in[rows, :]
        new_max, total = absorb(ready, old_max, vs[...])
        factor = jnp.exp2((old_max - new_max) * EXP_SCALE)
        total = a_in[rows, :] * jnp.concatenate([factor, factor], axis=1) + total
        attended = (total[:, :DH] / total[:, DH:]).astype(BF16)
        first = pl.multiple_of(step * HALF + t * TILE, TILE)
        for g in range(GROUPS):
            att[pl.ds(first, TILE), g * DH : (g + 1) * DH] = attended[
                g * TILE : (g + 1) * TILE
            ]
        ready = following

    @pl.when(step == 1)
    def _():
        for c in range(W_CHUNKS):
            w_copy(c).wait()
            window = slice(c * cols, (c + 1) * cols)
            term = jnp.dot(att[...], w_vmem[:, window], preferred_element_type=F32)
            term = term.astype(BF16)
            for i, out in enumerate(outs):
                out[:, window] = term[i * TILE : (i + 1) * TILE]


def params(mebibytes):
    return pltpu.CompilerParams(
        vmem_limit_bytes=mebibytes * 2**20, dimension_semantics=("arbitrary",)
    )


def cost(keys, rows=ROWS, extra=0):
    work = rows * GROUPS * keys
    return pl.CostEstimate(
        flops=8 * DH * work + extra, bytes_accessed=6 * 2**20, transcendentals=work
    )


def whole(shape):
    return pl.BlockSpec(shape, lambda i, meta: (0,) * len(shape))


def own_call(meta, lengths, q, cache, fresh):
    keys = TILE // STEPS * CACHE + HALF
    cache_rows = HALF // STEPS * CACHE
    return pl.pallas_call(
        own_kernel,
        grid_spec=pltpu.PrefetchScalarGridSpec(
            num_scalar_prefetch=1,
            grid=(ROWS // HALF,),
            in_specs=[
                pl.BlockSpec((1, 1, HALF), lambda i, meta: (i, 0, 0)),
                pl.BlockSpec((HALF, GROUPS * DH), lambda i, meta: (i, 0)),
                pl.BlockSpec((cache_rows, 2 * DH), lambda i, meta: (i, 0)),
                pl.BlockSpec((HALF, 2 * DH), lambda i, meta: (i, 0)),
            ],
            out_specs=[
                pl.BlockSpec((HALF * GROUPS, DH), lambda i, meta: (i, 0)),
                pl.BlockSpec((HALF * GROUPS, 2 * DH), lambda i, meta: (i, 0)),
            ],
            scratch_shapes=[
                pltpu.VMEM((2, 2 * DH, keys), BF16),
                pltpu.VMEM((2, keys, 2 * DH), BF16),
            ],
        ),
        out_shape=[
            jax.ShapeDtypeStruct((ROWS * GROUPS, DH), F32),
            jax.ShapeDtypeStruct((ROWS * GROUPS, 2 * DH), F32),
        ],
        compiler_params=params(20),
        cost_estimate=cost(keys),
        name="own_keys",
    )(meta, lengths, q, cache, fresh)


def prefix_call(name, plan, meta, pos, q, parts, state):
    n_parts = len(parts)
    keys = sum(p.shape[0] for p in parts)
    state_specs = [
        pl.BlockSpec((HALF * GROUPS, DH), lambda i, meta: (i, 0)),
        pl.BlockSpec((HALF * GROUPS, 2 * DH), lambda i, meta: (i, 0)),
    ]
    return pl.pallas_call(
        functools.partial(prefix_kernel, n_parts, plan),
        grid_spec=pltpu.PrefetchScalarGridSpec(
            num_scalar_prefetch=1,
            grid=(ROWS // HALF,),
            in_specs=[
                whole(pos.shape),
                pl.BlockSpec((HALF, GROUPS * DH), lambda i, meta: (i, 0)),
            ]
            + [whole(p.shape) for p in parts]
            + state_specs,
            out_specs=state_specs,
            scratch_shapes=[
                pltpu.VMEM((2 * DH, keys), BF16),
                pltpu.VMEM((keys, 2 * DH), BF16),
            ],
        ),
        out_shape=[jax.ShapeDtypeStruct(s.shape, F32) for s in state],
        input_output_aliases={3 + n_parts: 0, 4 + n_parts: 1},
        compiler_params=params(20),
        cost_estimate=cost(keys),
        name=name,
    )(meta, pos, q, *parts, *state)


def last_call(name, plan, meta, pos, q, parts, state, out_weight):
    n_parts = len(parts)
    keys = sum(p.shape[0] for p in parts)
    width = out_weight.shape[1]
    return pl.pallas_call(
        functools.partial(last_kernel, n_parts, plan),
        grid_spec=pltpu.PrefetchScalarGridSpec(
            num_scalar_prefetch=1,
            grid=(ROWS // HALF,),
            in_specs=[
                whole(pos.shape),
                pl.BlockSpec((HALF, GROUPS * DH), lambda i, meta: (meta[3] ^ i, 0)),
            ]
            + [whole(p.shape) for p in parts]
            + [
                pl.BlockSpec((HALF * GROUPS, DH), lambda i, meta: (meta[3] ^ i, 0)),
                pl.BlockSpec((HALF * GROUPS, 2 * DH), lambda i, meta: (meta[3] ^ i, 0)),
                pl.BlockSpec(memory_space=pl.ANY),
            ],
            out_specs=[whole((TILE, width))] * len(PLACES),
            scratch_shapes=[
                pltpu.VMEM((2 * DH, keys), BF16),
                pltpu.VMEM((keys, 2 * DH), BF16),
                pltpu.VMEM((ROWS, GROUPS * DH), BF16),
                pltpu.VMEM(out_weight.shape, BF16),
                pltpu.SemaphoreType.DMA((W_CHUNKS,)),
            ],
        ),
        out_shape=[jax.ShapeDtypeStruct((TILE, width), BF16)] * len(PLACES),
        compiler_params=params(36),
        cost_estimate=cost(keys, ROWS, 2 * ROWS * out_weight.size),
        name=name,
    )(meta, pos, q, *parts, *state, out_weight)


def on_device(queries, fresh_kv, positions, cache_kv, cache_lengths, out_weight):
    q = queries[0]
    own_kv = fresh_kv[0]
    section = lax.axis_index("section")
    seq = lax.axis_index("seq")
    head = lax.axis_index("head")

    meta = jnp.stack([section, seq >> 2, seq & 3, 1 - (head >> 2), head & 3])
    pos = positions.astype(F32).reshape(2 * 16, 1, HALF)
    lengths = jnp.repeat(cache_lengths, STEPS).astype(F32).reshape(2, 1, HALF)
    cache = cache_kv.reshape(ROWS // STEPS * CACHE, 2 * DH)

    other_kv = lax.ppermute(own_kv, "section", SWAP)
    mine = jnp.where(section == 0, own_kv[:HALF], other_kv[HALF:])
    blocks = [mine] + [lax.ppermute(mine, "seq", seq_perm(0, d)) for d in Z_ORDER[1:]]
    own_inputs = lax.optimization_barrier((mine, meta, lengths, pos))
    _, meta, lengths, pos = own_inputs
    state = own_call(meta, lengths, q, cache, own_kv)
    blocks[3], state = lax.optimization_barrier((blocks[3], state))
    near = jnp.concatenate(blocks, axis=0)
    far = {d: lax.ppermute(near, "seq", seq_perm(d, 0)) for d in (1, 3, 2)}
    near_swapped = lax.ppermute(near, "section", SWAP)
    state = prefix_call("near_keys", NEAR, meta, pos, q, [near, near_swapped], state)
    far[1], far[3], state = lax.optimization_barrier((far[1], far[3], state))
    sides = [far[1], far[3]] + [lax.ppermute(far[d], "section", SWAP) for d in (1, 3)]
    state = prefix_call("side_keys", SIDES, meta, pos, q, sides, state)
    far[2], state = lax.optimization_barrier((far[2], state))
    across = [far[2], lax.ppermute(far[2], "section", SWAP)]
    terms = last_call("across_keys", ACROSS, meta, pos, q, across, state, out_weight)
    terms = dict(zip(PLACES, terms))

    def move(term, dz, dx):
        return lax.ppermute(term, "head", head_perm(dz, dx))

    crossed = move(terms[1, 2], 1, 0)
    left_mirror = move(terms[1, 1], 0, 1)
    right_mirror = move(terms[1, 3], 0, 3)
    left = move(terms[0, 1], 0, 1)
    right = move(terms[0, 3], 0, 3)
    opposite = move(added(crossed, terms[0, 2]), 0, 2)
    mirror = move(added(left_mirror, right_mirror, terms[1, 0]), 1, 0)
    return added(terms[0, 0], left, right, opposite, mirror)[None]


def added(first, *others):
    total = first.astype(F32)
    for other in others:
        total = total + other.astype(F32)
    return total.astype(BF16)


def solution(mesh):
    in_specs = (
        P("section", "seq", "head"),
        P("section", "seq", "head"),
        P(),
        P("seq", None, "head"),
        P("seq"),
        P("head", None),
    )
    out_specs = P("section", ("seq", "head"), None)
    return jax.shard_map(
        on_device, mesh=mesh, in_specs=in_specs, out_specs=out_specs, check_vma=False
    )
```

```python
import functools
import math

import jax
import jax.numpy as jnp
from jax import lax
from jax.experimental import pallas as pl
from jax.experimental.pallas import tpu as pltpu
from jax.sharding import PartitionSpec as P

HQ = 64
KVH = 8
DH = 128
STEPS = 2
CACHE = 32
GROUPS = HQ // KVH
ROWS = 256
HALF = 128
TILE = 32
LHS = TILE * GROUPS
NEG = -1e30
BIG = float(2**22)
EXP_SCALE = DH**-0.5 * math.log2(math.e)
BF16 = jnp.bfloat16
F32 = jnp.float32
Z_ORDER = (0, 2, 1, 3)


W_CHUNKS = 8


def seq_perm(dy, dz):
    return [
        (y * 4 + z, ((y + dy) % 4) * 4 + (z + dz) % 4)
        for y in range(4)
        for z in range(4)
    ]


def head_perm(dz, dx):
    return [
        (z * 4 + x, (z ^ dz) * 4 + (x + dx) % 4)
        for z in range(2)
        for x in range(4)
    ]


SWAP = [(0, 1), (1, 0)]
NEAR = ((0, 0), (0, 1))
SIDES = ((1, 0), (3, 0), (1, 1), (3, 1))
ACROSS = ((2, 0), (2, 1))
PLACES_A = ((1, 2), (1, 1), (1, 3), (0, 2))
PLACES_B = ((1, 0), (0, 1), (0, 3), (0, 0))


def stacked_queries(q_ref, first_row, first_col):
    stack = jnp.concatenate(
        [q_ref[pl.ds(first_row, TILE), g * DH : (g + 1) * DH] for g in range(GROUPS)],
        axis=0,
    )
    rows = lax.broadcasted_iota(jnp.int32, (LHS, HALF), 0)
    cols = lax.broadcasted_iota(jnp.int32, (LHS, HALF), 1)
    marks = jnp.where((rows & (TILE - 1)) + first_col == cols, -BIG, 0.0).astype(BF16)
    return jnp.concatenate([stack, marks], axis=1)


def column_of(row, repeat=1, first=0):
    row = row.astype(F32)
    rows = lax.broadcasted_iota(jnp.int32, (HALF, HALF), 0) // repeat + first
    cols = lax.broadcasted_iota(jnp.int32, (HALF, HALF), 1)
    spread = jnp.where(rows == cols, jnp.broadcast_to(row, (HALF, HALF)), 0.0)
    return jnp.sum(spread, axis=1, keepdims=True)


def absorb(scores, old_max, values):
    width = scores.shape[1]
    top = scores[:, :DH]
    for j in range(DH, width, DH):
        top = jnp.maximum(top, scores[:, j : j + DH])
    new_max = jnp.max(top, axis=1, keepdims=True)
    if old_max is not None:
        new_max = jnp.maximum(old_max, new_max)
    else:
        new_max = jnp.broadcast_to(new_max, (LHS, DH))
    wide = jnp.concatenate([new_max] * (width // DH), axis=1)
    weights = jnp.exp2((scores - wide) * EXP_SCALE).astype(BF16)
    return new_max, jnp.dot(weights, values, preferred_element_type=F32)


def own_kernel(meta, len_ref, q_ref, cache_ref, fresh_ref, m_out, a_out, kt, vs):
    keys = TILE // STEPS * CACHE

    @pl.when(meta[0] == 0)
    def _():
        m_out[...] = jnp.full(m_out.shape, NEG, F32)
        a_out[...] = jnp.zeros(a_out.shape, F32)

    @pl.when(meta[0] == 1)
    def _():
        lengths = column_of(len_ref[...], STEPS, pl.program_id(0) * (HALF // STEPS))
        row = lax.broadcasted_iota(jnp.int32, (TILE, keys), 0)
        key = lax.broadcasted_iota(jnp.int32, (TILE, keys), 1)
        same = (key // CACHE) == (row // STEPS)
        nth = (key % CACHE).astype(F32)
        frow = lax.broadcasted_iota(jnp.int32, (TILE, HALF), 0)
        fkey = lax.broadcasted_iota(jnp.int32, (TILE, HALF), 1)
        for t in range(HALF // TILE):
            slot = t % 2
            kt[slot, DH + TILE :, :] = jnp.zeros((DH - TILE, keys + HALF), BF16)
            kt[slot, :DH, :keys] = cache_ref[t * keys : (t + 1) * keys, :DH].T
            kt[slot, :DH, keys:] = fresh_ref[:, :DH].T
            seen = same & (nth < lengths[t * TILE : (t + 1) * TILE])
            kt[slot, DH : DH + TILE, :keys] = jnp.where(seen, 0.0, 1.0).astype(BF16)
            mine = frow + t * TILE
            seen = ((mine // STEPS) == (fkey // STEPS)) & (fkey <= mine)
            kt[slot, DH : DH + TILE, keys:] = jnp.where(seen, 0.0, 1.0).astype(BF16)
            vs[slot, :keys, :DH] = cache_ref[t * keys : (t + 1) * keys, DH:]
            vs[slot, keys:, :DH] = fresh_ref[:, DH:]
            vs[slot, :, DH:] = jnp.ones((keys + HALF, DH), BF16)
            lhs = stacked_queries(q_ref, t * TILE, 0)
            scores = jnp.dot(lhs, kt[slot], preferred_element_type=F32)
            new_max, total = absorb(scores, None, vs[slot])
            m_out[t * LHS : (t + 1) * LHS, :] = new_max
            a_out[t * LHS : (t + 1) * LHS, :] = total


def load_keys(parts, kt, vs):
    count = parts[0].shape[0]
    for i, part in enumerate(parts):
        kt[0, :, i * count : (i + 1) * count] = part[:, :DH].T
        vs[i * count : (i + 1) * count, :DH] = part[:, DH:]
    vs[:, DH:] = jnp.ones((len(parts) * count, DH), BF16)


def load_mask(meta, plan, block, pos_ref, kt):
    own = (meta[1] * 4 + meta[2]) * 2
    bound = jnp.where(meta[0] == 1, 1e9, column_of(pos_ref[own + block]))
    pieces = [(dy, dz, flip) for dy, flip in plan for dz in Z_ORDER]
    for j, (dy, dz, flip) in enumerate(pieces):
        source = ((meta[1] - dy) & 3) * 4 + ((meta[2] - dz) & 3)
        key_pos = pos_ref[source * 2 + (meta[0] ^ flip)].astype(F32)
        hidden = jnp.where(key_pos > bound, 1.0, 0.0).astype(BF16)
        kt[1 + block, :, j * HALF : (j + 1) * HALF] = hidden


def prefix_kernel(n_parts, plan, meta, pos_ref, q_ref, *refs):
    parts = refs[:n_parts]
    m_in, a_in, m_out, a_out, kt, vs = refs[n_parts:]
    load_keys(parts, kt, vs)
    for block in range(ROWS // HALF):
        load_mask(meta, plan, block, pos_ref, kt)
    tiles = ROWS // TILE

    def scores_of(t):
        return scores_at(q_ref, kt, t * TILE, t * TILE % HALF, t * TILE // HALF)

    ready = scores_of(0)
    for t in range(tiles):
        following = scores_of(t + 1) if t + 1 < tiles else None
        rows = slice(t * LHS, (t + 1) * LHS)
        new_max, total = fold_in(ready, m_in[rows, :], a_in[rows, :], vs)
        m_out[rows, :] = new_max
        a_out[rows, :] = total
        ready = following


def scores_at(q_ref, kt, first_row, first_col, block):
    lhs = stacked_queries(q_ref, first_row, first_col)
    keys = jnp.concatenate([kt[0], kt[1 + block]], axis=0)
    return jnp.dot(lhs, keys, preferred_element_type=F32)


def fold_in(scores, old_max, old_total, vs):
    new_max, total = absorb(scores, old_max, vs[...])
    factor = jnp.exp2((old_max - new_max) * EXP_SCALE)
    return new_max, old_total * jnp.concatenate([factor, factor], axis=1) + total


def last_kernel(n_parts, plan, places, meta, pos_ref, q_ref, *refs):
    parts = refs[:n_parts]
    m_in, a_in, w_ref = refs[n_parts : n_parts + 3]
    outs = refs[n_parts + 3 : n_parts + 3 + len(places)]
    kt, vs, att = refs[n_parts + 3 + len(places) :]
    cols = w_ref.shape[1] // W_CHUNKS
    load_keys(parts, kt, vs)
    for block in range(ROWS // HALF):
        load_mask(meta, plan, block, pos_ref, kt)
    tiles = HALF // TILE

    def place_of(t):
        dz, dx = places[t]
        return meta[3] ^ dz, (meta[4] + dx) & (tiles - 1)

    def scores_of(t):
        block, tile = place_of(t)
        first_col = pl.multiple_of(tile * TILE, TILE)
        first_row = pl.multiple_of(block * HALF + first_col, TILE)
        return scores_at(q_ref, kt, first_row, first_col, block)

    ready = scores_of(0)
    for t in range(len(places)):
        following = scores_of(t + 1) if t + 1 < len(places) else None
        block, tile = place_of(t)
        rows = pl.ds(pl.multiple_of((block * tiles + tile) * LHS, LHS), LHS)
        _, total = fold_in(ready, m_in[rows, :], a_in[rows, :], vs)
        attended = (total[:, :DH] / total[:, DH:]).astype(BF16)
        for g in range(GROUPS):
            att[t * TILE : (t + 1) * TILE, g * DH : (g + 1) * DH] = attended[
                g * TILE : (g + 1) * TILE
            ]
        ready = following
    for c in range(W_CHUNKS):
        window = slice(c * cols, (c + 1) * cols)
        term = jnp.dot(att[...], w_ref[:, window], preferred_element_type=F32)
        term = term.astype(BF16)
        for t in range(len(places)):
            outs[t][:, window] = term[t * TILE : (t + 1) * TILE]


def params(mebibytes):
    return pltpu.CompilerParams(vmem_limit_bytes=mebibytes * 2**20)


def cost(keys, rows=ROWS, extra=0):
    work = rows * GROUPS * keys
    return pl.CostEstimate(
        flops=8 * DH * work + extra, bytes_accessed=6 * 2**20, transcendentals=work
    )


def whole(shape):
    return pl.BlockSpec(shape, lambda i, meta: (0,) * len(shape))


def own_call(meta, lengths, q, cache, fresh):
    keys = TILE // STEPS * CACHE + HALF
    cache_rows = HALF // STEPS * CACHE
    return pl.pallas_call(
        own_kernel,
        grid_spec=pltpu.PrefetchScalarGridSpec(
            num_scalar_prefetch=1,
            grid=(ROWS // HALF,),
            in_specs=[
                whole((1, HALF)),
                pl.BlockSpec((HALF, GROUPS * DH), lambda i, meta: (i, 0)),
                pl.BlockSpec((cache_rows, 2 * DH), lambda i, meta: (i, 0)),
                pl.BlockSpec((HALF, 2 * DH), lambda i, meta: (i, 0)),
            ],
            out_specs=[
                pl.BlockSpec((HALF * GROUPS, DH), lambda i, meta: (i, 0)),
                pl.BlockSpec((HALF * GROUPS, 2 * DH), lambda i, meta: (i, 0)),
            ],
            scratch_shapes=[
                pltpu.VMEM((2, 2 * DH, keys), BF16),
                pltpu.VMEM((2, keys, 2 * DH), BF16),
            ],
        ),
        out_shape=[
            jax.ShapeDtypeStruct((ROWS * GROUPS, DH), F32),
            jax.ShapeDtypeStruct((ROWS * GROUPS, 2 * DH), F32),
        ],
        compiler_params=params(20),
        cost_estimate=cost(keys),
        name="own_keys",
    )(meta, lengths, q, cache, fresh)


VMEM = pl.BlockSpec(memory_space=pltpu.VMEM)
SMEM = pl.BlockSpec(memory_space=pltpu.SMEM)


def prefix_call(name, plan, meta, pos, q, parts, state):
    n_parts = len(parts)
    keys = sum(p.shape[0] for p in parts)
    return pl.pallas_call(
        functools.partial(prefix_kernel, n_parts, plan),
        in_specs=[SMEM] + [VMEM] * (4 + n_parts),
        out_specs=[VMEM] * 2,
        scratch_shapes=[
            pltpu.VMEM((1 + ROWS // HALF, DH, keys), BF16),
            pltpu.VMEM((keys, 2 * DH), BF16),
        ],
        out_shape=[jax.ShapeDtypeStruct(s.shape, F32) for s in state],
        input_output_aliases={3 + n_parts: 0, 4 + n_parts: 1},
        compiler_params=params(20),
        cost_estimate=cost(keys),
        name=name,
    )(meta, pos, q, *parts, *state)


def last_call(name, plan, places, meta, pos, q, parts, state, out_weight):
    n_parts = len(parts)
    keys = sum(p.shape[0] for p in parts)
    width = out_weight.shape[1]
    rows = TILE * len(places)
    terms = pl.pallas_call(
        functools.partial(last_kernel, n_parts, plan, places),
        in_specs=[SMEM] + [VMEM] * (5 + n_parts),
        out_specs=[VMEM] * len(places),
        scratch_shapes=[
            pltpu.VMEM((1 + ROWS // HALF, DH, keys), BF16),
            pltpu.VMEM((keys, 2 * DH), BF16),
            pltpu.VMEM((rows, GROUPS * DH), BF16),
        ],
        out_shape=[jax.ShapeDtypeStruct((TILE, width), BF16)] * len(places),
        compiler_params=params(20),
        cost_estimate=cost(keys, rows, 2 * rows * out_weight.size),
        name=name,
    )(meta, pos, q, *parts, *state, out_weight)
    return dict(zip(places, terms))


def on_device(queries, fresh_kv, positions, cache_kv, cache_lengths, out_weight):
    q = queries[0]
    own_kv = fresh_kv[0]
    section = lax.axis_index("section")
    seq = lax.axis_index("seq")
    head = lax.axis_index("head")

    meta = jnp.stack([section, seq >> 2, seq & 3, head >> 2, head & 3])
    pos = positions.reshape(-1, 1, HALF)
    lengths = cache_lengths.reshape(1, HALF)
    cache = cache_kv.reshape(ROWS // STEPS * CACHE, 2 * DH)

    other_kv = lax.ppermute(own_kv, "section", SWAP)
    mine = jnp.where(section == 0, own_kv[:HALF], other_kv[HALF:])
    blocks = [mine] + [lax.ppermute(mine, "seq", seq_perm(0, d)) for d in Z_ORDER[1:]]
    own_inputs = lax.optimization_barrier((mine, meta, lengths, pos))
    _, meta, lengths, pos = own_inputs
    state = own_call(meta, lengths, q, cache, own_kv)
    blocks[3], state = lax.optimization_barrier((blocks[3], state))
    near = jnp.concatenate(blocks, axis=0)
    far = {d: lax.ppermute(near, "seq", seq_perm(d, 0)) for d in (1, 3, 2)}
    near_swapped = lax.ppermute(near, "section", SWAP)
    state = prefix_call("near_keys", NEAR, meta, pos, q, [near, near_swapped], state)
    far[1], far[3], state = lax.optimization_barrier((far[1], far[3], state))
    sides = [far[1], far[3]] + [lax.ppermute(far[d], "section", SWAP) for d in (1, 3)]
    state = prefix_call("side_keys", SIDES, meta, pos, q, sides, state)
    far[2], state = lax.optimization_barrier((far[2], state))
    across = [far[2], lax.ppermute(far[2], "section", SWAP)]
    across = (ACROSS, meta, pos, q, across, state, out_weight)
    terms = last_call("across_keys_a", across[0], PLACES_A, *across[1:])
    terms.update(last_call("across_keys_b", across[0], PLACES_B, *across[1:]))

    def move(term, dz, dx):
        return lax.ppermute(term, "head", head_perm(dz, dx))

    crossed = move(terms[1, 2], 1, 0)
    left_mirror = move(terms[1, 1], 0, 1)
    right_mirror = move(terms[1, 3], 0, 3)
    left = move(terms[0, 1], 0, 1)
    right = move(terms[0, 3], 0, 3)
    opposite = move(added(crossed, terms[0, 2]), 0, 2)
    mirror = move(added(left_mirror, right_mirror, terms[1, 0]), 1, 0)
    return added(terms[0, 0], left, right, opposite, mirror)[None]


def added(first, *others):
    total = first.astype(F32)
    for other in others:
        total = total + other.astype(F32)
    return total.astype(BF16)


def solution(mesh):
    in_specs = (
        P("section", "seq", "head"),
        P("section", "seq", "head"),
        P(),
        P("seq", None, "head"),
        P("seq"),
        P("head", None),
    )
    out_specs = P("section", ("seq", "head"), None)
    return jax.shard_map(
        on_device, mesh=mesh, in_specs=in_specs, out_specs=out_specs, check_vma=False
    )
```

```python
import functools
import math

import jax
import jax.numpy as jnp
from jax import lax
from jax.experimental import pallas as pl
from jax.experimental.pallas import tpu as pltpu
from jax.sharding import PartitionSpec as P

HQ = 64
KVH = 8
DH = 128
STEPS = 2
CACHE = 32
GROUPS = HQ // KVH
ROWS = 256
HALF = 128
TILE = 32
LHS = TILE * GROUPS
NEG = -1e30
BIG = float(2**22)
EXP_SCALE = DH**-0.5 * math.log2(math.e)
BF16 = jnp.bfloat16
F32 = jnp.float32
Z_ORDER = (0, 2, 1, 3)


W_CHUNKS = 8
SLOTS = 4


def seq_perm(dy, dz):
    return [
        (y * 4 + z, ((y + dy) % 4) * 4 + (z + dz) % 4)
        for y in range(4)
        for z in range(4)
    ]


def head_perm(dz, dx):
    return [
        (z * 4 + x, (z ^ dz) * 4 + (x + dx) % 4)
        for z in range(2)
        for x in range(4)
    ]


SWAP = [(0, 1), (1, 0)]
NEAR = ((0, 0), (0, 1))
SIDES = ((1, 0), (3, 0))
OTHER_SIDES = ((1, 1), (3, 1))
ACROSS = ((2, 0), (2, 1))
PLACES_A = ((1, 2), (1, 1), (1, 3), (0, 2))
PLACES_B = ((1, 0), (0, 1), (0, 3), (0, 0))


def stacked_queries(q_ref, first_row, first_col):
    stack = jnp.concatenate(
        [q_ref[pl.ds(first_row, TILE), g * DH : (g + 1) * DH] for g in range(GROUPS)],
        axis=0,
    )
    rows = lax.broadcasted_iota(jnp.int32, (LHS, HALF), 0)
    cols = lax.broadcasted_iota(jnp.int32, (LHS, HALF), 1)
    marks = jnp.where((rows & (TILE - 1)) + first_col == cols, -BIG, 0.0).astype(BF16)
    return jnp.concatenate([stack, marks], axis=1)


def column_of(row, repeat=1, first=0):
    row = row.astype(F32)
    rows = lax.broadcasted_iota(jnp.int32, (HALF, HALF), 0) // repeat + first
    cols = lax.broadcasted_iota(jnp.int32, (HALF, HALF), 1)
    spread = jnp.where(rows == cols, jnp.broadcast_to(row, (HALF, HALF)), 0.0)
    return jnp.sum(spread, axis=1, keepdims=True)


def absorb(scores, old_max, values):
    width = scores.shape[1]
    top = scores[:, :DH]
    for j in range(DH, width, DH):
        top = jnp.maximum(top, scores[:, j : j + DH])
    new_max = jnp.max(top, axis=1, keepdims=True)
    if old_max is not None:
        new_max = jnp.maximum(old_max, new_max)
    else:
        new_max = jnp.broadcast_to(new_max, (LHS, DH))
    wide = jnp.concatenate([new_max] * (width // DH), axis=1)
    weights = jnp.exp2((scores - wide) * EXP_SCALE).astype(BF16)
    return new_max, jnp.dot(weights, values, preferred_element_type=F32)


def own_kernel(
    meta, len_ref, q_hbm, cache_hbm, fresh_hbm, m_out, a_out, kt, vs, q_ref, cache_ref, fresh_ref, sems
):
    keys = TILE // STEPS * CACHE
    tiles = ROWS // TILE

    @pl.when(meta[0] == 0)
    def _():
        m_out[...] = jnp.full(m_out.shape, NEG, F32)
        a_out[...] = jnp.zeros(a_out.shape, F32)

    @pl.when(meta[0] == 1)
    def _():
        def cache_copy(t):
            window = pl.ds(t * keys, keys)
            return pltpu.make_async_copy(
                cache_hbm.at[window], cache_ref.at[window], sems.at[2 + t]
            )

        fresh_copy = pltpu.make_async_copy(fresh_hbm, fresh_ref, sems.at[0])
        q_copy = pltpu.make_async_copy(q_hbm, q_ref, sems.at[1])
        fresh_copy.start()
        cache_copy(0).start()
        q_copy.start()
        for t in range(1, tiles):
            cache_copy(t).start()
        row = lax.broadcasted_iota(jnp.int32, (TILE, keys), 0)
        key = lax.broadcasted_iota(jnp.int32, (TILE, keys), 1)
        same = (key // CACHE) == (row // STEPS)
        nth = (key % CACHE).astype(F32)
        frow = lax.broadcasted_iota(jnp.int32, (TILE, HALF), 0)
        fkey = lax.broadcasted_iota(jnp.int32, (TILE, HALF), 1)
        for slot in range(SLOTS):
            kt[slot, DH + TILE :, :] = jnp.zeros((DH - TILE, keys + HALF), BF16)
            vs[slot, :, DH:] = jnp.ones((keys + HALF, DH), BF16)
        fresh_copy.wait()
        for t in range(tiles):
            slot = t % SLOTS
            block, mine = t * TILE // HALF, frow + t * TILE % HALF
            if t * TILE % HALF == 0:
                lengths = column_of(len_ref[...], STEPS, block * (HALF // STEPS))
                fresh = slice(block * HALF, (block + 1) * HALF)
                for at in range(SLOTS):
                    kt[at, :DH, keys:] = fresh_ref[fresh, :DH].T
                    vs[at, keys:, :DH] = fresh_ref[fresh, DH:]
            if t == 0:
                q_copy.wait()
            if t % SLOTS == 0:
                for ahead in range(t, t + SLOTS):
                    cache_copy(ahead).wait()
            kt[slot, :DH, :keys] = cache_ref[t * keys : (t + 1) * keys, :DH].T
            first = t * TILE % HALF
            seen = same & (nth < lengths[first : first + TILE])
            kt[slot, DH : DH + TILE, :keys] = jnp.where(seen, 0.0, 1.0).astype(BF16)
            seen = ((mine // STEPS) == (fkey // STEPS)) & (fkey <= mine)
            kt[slot, DH : DH + TILE, keys:] = jnp.where(seen, 0.0, 1.0).astype(BF16)
            vs[slot, :keys, :DH] = cache_ref[t * keys : (t + 1) * keys, DH:]
            lhs = stacked_queries(q_ref, t * TILE, 0)
            scores = jnp.dot(lhs, kt[slot], preferred_element_type=F32)
            new_max, total = absorb(scores, None, vs[slot])
            m_out[t * LHS : (t + 1) * LHS, :] = new_max
            a_out[t * LHS : (t + 1) * LHS, :] = total


def load_keys(parts, kt, vs):
    count = parts[0].shape[0]
    for i, part in enumerate(parts):
        kt[0, :, i * count : (i + 1) * count] = part[:, :DH].T
        vs[i * count : (i + 1) * count, :DH] = part[:, DH:]
    vs[:, DH:] = jnp.ones((len(parts) * count, DH), BF16)


def load_mask(meta, plan, block, pos_ref, kt):
    own = (meta[1] * 4 + meta[2]) * 2
    bound = jnp.where(meta[0] == 1, 1e9, column_of(pos_ref[own + block]))
    pieces = [(dy, dz, flip) for dy, flip in plan for dz in Z_ORDER]
    for j, (dy, dz, flip) in enumerate(pieces):
        source = ((meta[1] - dy) & 3) * 4 + ((meta[2] - dz) & 3)
        key_pos = pos_ref[source * 2 + (meta[0] ^ flip)].astype(F32)
        hidden = jnp.where(key_pos > bound, 1.0, 0.0).astype(BF16)
        kt[1 + block, :, j * HALF : (j + 1) * HALF] = hidden


def prefix_kernel(n_parts, plan, meta, pos_ref, q_ref, *refs):
    parts = refs[:n_parts]
    m_in, a_in, m_out, a_out, kt, vs = refs[n_parts:]
    load_keys(parts, kt, vs)
    for block in range(ROWS // HALF):
        load_mask(meta, plan, block, pos_ref, kt)
    tiles = ROWS // TILE

    def scores_of(t):
        return scores_at(q_ref, kt, t * TILE, t * TILE % HALF, t * TILE // HALF)

    ready = scores_of(0)
    for t in range(tiles):
        following = scores_of(t + 1) if t + 1 < tiles else None
        rows = slice(t * LHS, (t + 1) * LHS)
        new_max, total = fold_in(ready, m_in[rows, :], a_in[rows, :], vs)
        m_out[rows, :] = new_max
        a_out[rows, :] = total
        ready = following


def scores_at(q_ref, kt, first_row, first_col, block):
    lhs = stacked_queries(q_ref, first_row, first_col)
    keys = jnp.concatenate([kt[0], kt[1 + block]], axis=0)
    return jnp.dot(lhs, keys, preferred_element_type=F32)


def fold_in(scores, old_max, old_total, vs):
    new_max, total = absorb(scores, old_max, vs[...])
    factor = jnp.exp2((old_max - new_max) * EXP_SCALE)
    return new_max, old_total * jnp.concatenate([factor, factor], axis=1) + total


def last_kernel(n_parts, plan, places, meta, pos_ref, q_ref, *refs):
    parts = refs[:n_parts]
    m_in, a_in, w_ref = refs[n_parts : n_parts + 3]
    outs = refs[n_parts + 3 : n_parts + 3 + len(places)]
    kt, vs, att = refs[n_parts + 3 + len(places) :]
    cols = w_ref.shape[1] // W_CHUNKS
    load_keys(parts, kt, vs)
    for block in range(ROWS // HALF):
        load_mask(meta, plan, block, pos_ref, kt)
    tiles = HALF // TILE

    def place_of(t):
        dz, dx = places[t]
        return meta[3] ^ dz, (meta[4] + dx) & (tiles - 1)

    def scores_of(t):
        block, tile = place_of(t)
        first_col = pl.multiple_of(tile * TILE, TILE)
        first_row = pl.multiple_of(block * HALF + first_col, TILE)
        return scores_at(q_ref, kt, first_row, first_col, block)

    ready = scores_of(0)
    for t in range(len(places)):
        following = scores_of(t + 1) if t + 1 < len(places) else None
        block, tile = place_of(t)
        rows = pl.ds(pl.multiple_of((block * tiles + tile) * LHS, LHS), LHS)
        _, total = fold_in(ready, m_in[rows, :], a_in[rows, :], vs)
        attended = (total[:, :DH] / total[:, DH:]).astype(BF16)
        for g in range(GROUPS):
            att[t * TILE : (t + 1) * TILE, g * DH : (g + 1) * DH] = attended[
                g * TILE : (g + 1) * TILE
            ]
        ready = following
    for c in range(W_CHUNKS):
        window = slice(c * cols, (c + 1) * cols)
        term = jnp.dot(att[...], w_ref[:, window], preferred_element_type=F32)
        term = term.astype(BF16)
        for t in range(len(places)):
            outs[t][:, window] = term[t * TILE : (t + 1) * TILE]


def params(mebibytes):
    return pltpu.CompilerParams(vmem_limit_bytes=mebibytes * 2**20)


def cost(keys, rows=ROWS, extra=0):
    work = rows * GROUPS * keys
    return pl.CostEstimate(
        flops=8 * DH * work + extra, bytes_accessed=rows * 2**14, transcendentals=work
    )


VMEM = pl.BlockSpec(memory_space=pltpu.VMEM)
SMEM = pl.BlockSpec(memory_space=pltpu.SMEM)
HBM = pl.BlockSpec(memory_space=pltpu.HBM)


def own_call(meta, lengths, q, cache, fresh):
    keys = TILE // STEPS * CACHE + HALF
    return pl.pallas_call(
        own_kernel,
        in_specs=[SMEM, VMEM, HBM, HBM, HBM],
        out_specs=[VMEM] * 2,
        scratch_shapes=[
            pltpu.VMEM((SLOTS, 2 * DH, keys), BF16),
            pltpu.VMEM((SLOTS, keys, 2 * DH), BF16),
            pltpu.VMEM(q.shape, BF16),
            pltpu.VMEM(cache.shape, BF16),
            pltpu.VMEM(fresh.shape, BF16),
            pltpu.SemaphoreType.DMA((2 + ROWS // TILE,)),
        ],
        out_shape=[
            jax.ShapeDtypeStruct((ROWS * GROUPS, DH), F32),
            jax.ShapeDtypeStruct((ROWS * GROUPS, 2 * DH), F32),
        ],
        compiler_params=params(50),
        cost_estimate=cost(keys),
        name="own_keys",
    )(meta, lengths, q, cache, fresh)


def prefix_call(name, plan, meta, pos, q, parts, state, rows=ROWS):
    n_parts = len(parts)
    keys = sum(p.shape[0] for p in parts)
    return pl.pallas_call(
        functools.partial(prefix_kernel, n_parts, plan),
        in_specs=[SMEM] + [VMEM] * (4 + n_parts),
        out_specs=[VMEM] * 2,
        scratch_shapes=[
            pltpu.VMEM((1 + ROWS // HALF, DH, keys), BF16),
            pltpu.VMEM((keys, 2 * DH), BF16),
        ],
        out_shape=[jax.ShapeDtypeStruct(s.shape, F32) for s in state],
        input_output_aliases={3 + n_parts: 0, 4 + n_parts: 1},
        compiler_params=params(20),
        cost_estimate=cost(keys, rows),
        name=name,
    )(meta, pos, q, *parts, *state)


def last_call(name, plan, places, meta, pos, q, parts, state, out_weight):
    n_parts = len(parts)
    keys = sum(p.shape[0] for p in parts)
    width = out_weight.shape[1]
    rows = TILE * len(places)
    terms = pl.pallas_call(
        functools.partial(last_kernel, n_parts, plan, places),
        in_specs=[SMEM] + [VMEM] * (5 + n_parts),
        out_specs=[VMEM] * len(places),
        scratch_shapes=[
            pltpu.VMEM((1 + ROWS // HALF, DH, keys), BF16),
            pltpu.VMEM((keys, 2 * DH), BF16),
            pltpu.VMEM((rows, GROUPS * DH), BF16),
        ],
        out_shape=[jax.ShapeDtypeStruct((TILE, width), BF16)] * len(places),
        compiler_params=params(20),
        cost_estimate=cost(keys, rows, 2 * rows * out_weight.size),
        name=name,
    )(meta, pos, q, *parts, *state, out_weight)
    return dict(zip(places, terms))


def on_device(queries, fresh_kv, positions, cache_kv, cache_lengths, out_weight):
    q = queries[0]
    own_kv = fresh_kv[0]
    section = lax.axis_index("section")
    seq = lax.axis_index("seq")
    head = lax.axis_index("head")

    meta = jnp.stack([section, seq >> 2, seq & 3, head >> 2, head & 3])
    pos = positions.reshape(-1, 1, HALF)
    lengths = cache_lengths.reshape(1, HALF)
    cache = cache_kv.reshape(ROWS // STEPS * CACHE, 2 * DH)

    other_kv = lax.ppermute(own_kv, "section", SWAP)
    mine = jnp.where(section == 0, own_kv[:HALF], other_kv[HALF:])
    blocks = [mine] + [lax.ppermute(mine, "seq", seq_perm(0, d)) for d in Z_ORDER[1:]]
    own_inputs = lax.optimization_barrier((mine, meta, lengths, pos))
    _, meta, lengths, pos = own_inputs
    state = own_call(meta, lengths, q, cache, own_kv)
    blocks[3], state = lax.optimization_barrier((blocks[3], state))
    near = jnp.concatenate(blocks, axis=0)
    far = {d: lax.ppermute(near, "seq", seq_perm(d, 0)) for d in (1, 3)}
    near_swapped = lax.ppermute(near, "section", SWAP)
    state = prefix_call("near_keys", NEAR, meta, pos, q, [near, near_swapped], state)
    sent, state = lax.optimization_barrier((near, state))
    far[2] = lax.ppermute(sent, "seq", seq_perm(2, 0))
    far[1], far[3], state = lax.optimization_barrier((far[1], far[3], state))
    swapped = {d: lax.ppermute(far[d], "section", SWAP) for d in (1, 3)}
    state = prefix_call("side_keys", SIDES, meta, pos, q, [far[1], far[3]], state, 1)
    far[2], state = lax.optimization_barrier((far[2], state))
    swapped[2] = lax.ppermute(far[2], "section", SWAP)
    others = [swapped[1], swapped[3]]
    state = prefix_call("other_side_keys", OTHER_SIDES, meta, pos, q, others, state)
    across = [far[2], swapped[2]]
    across = (ACROSS, meta, pos, q, across, state, out_weight)
    terms = last_call("across_keys_a", across[0], PLACES_A, *across[1:])
    terms.update(last_call("across_keys_b", across[0], PLACES_B, *across[1:]))

    def move(term, dz, dx):
        return lax.ppermute(term, "head", head_perm(dz, dx))

    crossed = move(terms[1, 2], 1, 0)
    left_mirror = move(terms[1, 1], 0, 1)
    right_mirror = move(terms[1, 3], 0, 3)
    left = move(terms[0, 1], 0, 1)
    right = move(terms[0, 3], 0, 3)
    opposite = move(added(crossed, terms[0, 2]), 0, 2)
    mirror = move(added(left_mirror, right_mirror, terms[1, 0]), 1, 0)
    return added(terms[0, 0], left, right, opposite, mirror)[None]


def added(first, *others):
    total = first.astype(F32)
    for other in others:
        total = total + other.astype(F32)
    return total.astype(BF16)


def solution(mesh):
    in_specs = (
        P("section", "seq", "head"),
        P("section", "seq", "head"),
        P(),
        P("seq", None, "head"),
        P("seq"),
        P("head", None),
    )
    out_specs = P("section", ("seq", "head"), None)
    return jax.shard_map(
        on_device, mesh=mesh, in_specs=in_specs, out_specs=out_specs, check_vma=False
    )
```

```python
import functools
import math

import jax
import jax.numpy as jnp
from jax import lax
from jax.experimental import pallas as pl
from jax.experimental.pallas import tpu as pltpu
from jax.sharding import PartitionSpec as P

HQ = 64
KVH = 8
DH = 128
STEPS = 2
CACHE = 32
GROUPS = HQ // KVH
ROWS = 256
HALF = 128
TILE = 32
OWN_TILE = 16
LHS = TILE * GROUPS
NEG = -1e30
BIG = float(2**22)
EXP_SCALE = DH**-0.5 * math.log2(math.e)
BF16 = jnp.bfloat16
F32 = jnp.float32
Z_ORDER = (0, 2, 1, 3)


W_CHUNKS = 8
SLOTS = 8


def seq_perm(dy, dz):
    return [
        (y * 4 + z, ((y + dy) % 4) * 4 + (z + dz) % 4)
        for y in range(4)
        for z in range(4)
    ]


def head_perm(dz, dx):
    return [
        (z * 4 + x, (z ^ dz) * 4 + (x + dx) % 4)
        for z in range(2)
        for x in range(4)
    ]


SWAP = [(0, 1), (1, 0)]
NEAR = ((0, 0), (0, 1))
SIDES = ((1, 0), (3, 0))
REST = ((1, 1), (3, 1), (2, 0), (2, 1))
PLACES_A = ((1, 2), (1, 1), (1, 3), (0, 1), (0, 3))
PLACES_B = ((0, 2), (1, 0), (0, 0))


def stacked_queries(q_ref, first_row, first_col, tile=TILE):
    stack = jnp.concatenate(
        [q_ref[pl.ds(first_row, tile), g * DH : (g + 1) * DH] for g in range(GROUPS)],
        axis=0,
    )
    rows = lax.broadcasted_iota(jnp.int32, (tile * GROUPS, HALF), 0)
    cols = lax.broadcasted_iota(jnp.int32, (tile * GROUPS, HALF), 1)
    marks = jnp.where((rows & (tile - 1)) + first_col == cols, -BIG, 0.0).astype(BF16)
    return jnp.concatenate([stack, marks], axis=1)


def column_of(row, repeat=1, first=0):
    row = row.astype(F32)
    rows = lax.broadcasted_iota(jnp.int32, (HALF, HALF), 0) // repeat + first
    cols = lax.broadcasted_iota(jnp.int32, (HALF, HALF), 1)
    spread = jnp.where(rows == cols, jnp.broadcast_to(row, (HALF, HALF)), 0.0)
    return jnp.sum(spread, axis=1, keepdims=True)


def absorb(scores, old_max, values):
    width = scores.shape[1]
    top = scores[:, :DH]
    for j in range(DH, width, DH):
        top = jnp.maximum(top, scores[:, j : j + DH])
    new_max = jnp.max(top, axis=1, keepdims=True)
    if old_max is not None:
        new_max = jnp.maximum(old_max, new_max)
    else:
        new_max = jnp.broadcast_to(new_max, (scores.shape[0], DH))
    wide = jnp.concatenate([new_max] * (width // DH), axis=1)
    weights = jnp.exp2((scores - wide) * EXP_SCALE).astype(BF16)
    return new_max, jnp.dot(weights, values, preferred_element_type=F32)


def own_kernel(
    meta, len_ref, q_hbm, cache_hbm, fresh_hbm, m_out, a_out, kt, vs, q_ref, cache_ref, fresh_ref, sems
):
    keys = OWN_TILE // STEPS * CACHE
    tiles = ROWS // OWN_TILE

    @pl.when(meta[0] == 0)
    def _():
        m_out[...] = jnp.full(m_out.shape, NEG, F32)
        a_out[...] = jnp.zeros(a_out.shape, F32)

    @pl.when(meta[0] == 1)
    def _():
        def cache_copy(t):
            window = pl.ds(t * keys, keys)
            return pltpu.make_async_copy(
                cache_hbm.at[window], cache_ref.at[window], sems.at[2 + t]
            )

        fresh_copy = pltpu.make_async_copy(fresh_hbm, fresh_ref, sems.at[0])
        q_copy = pltpu.make_async_copy(q_hbm, q_ref, sems.at[1])
        fresh_copy.start()
        cache_copy(0).start()
        q_copy.start()
        for t in range(1, tiles):
            cache_copy(t).start()
        row = lax.broadcasted_iota(jnp.int32, (OWN_TILE, keys), 0)
        key = lax.broadcasted_iota(jnp.int32, (OWN_TILE, keys), 1)
        same = (key // CACHE) == (row // STEPS)
        nth = (key % CACHE).astype(F32)
        frow = lax.broadcasted_iota(jnp.int32, (OWN_TILE, HALF), 0)
        fkey = lax.broadcasted_iota(jnp.int32, (OWN_TILE, HALF), 1)
        for slot in range(SLOTS):
            kt[slot, DH + OWN_TILE :, :] = jnp.zeros((DH - OWN_TILE, keys + HALF), BF16)
            vs[slot, :, DH:] = jnp.ones((keys + HALF, DH), BF16)
        fresh_copy.wait()
        for t in range(tiles):
            slot = t % SLOTS
            block, mine = t * OWN_TILE // HALF, frow + t * OWN_TILE % HALF
            if t * OWN_TILE % HALF == 0:
                lengths = column_of(len_ref[...], STEPS, block * (HALF // STEPS))
                fresh = slice(block * HALF, (block + 1) * HALF)
                for at in range(SLOTS):
                    kt[at, :DH, keys:] = fresh_ref[fresh, :DH].T
                    vs[at, keys:, :DH] = fresh_ref[fresh, DH:]
            if t == 0:
                q_copy.wait()
            if t % SLOTS == 0:
                for ahead in range(t, t + SLOTS):
                    cache_copy(ahead).wait()
            kt[slot, :DH, :keys] = cache_ref[t * keys : (t + 1) * keys, :DH].T
            first = t * OWN_TILE % HALF
            seen = same & (nth < lengths[first : first + OWN_TILE])
            kt[slot, DH : DH + OWN_TILE, :keys] = jnp.where(seen, 0.0, 1.0).astype(BF16)
            seen = ((mine // STEPS) == (fkey // STEPS)) & (fkey <= mine)
            kt[slot, DH : DH + OWN_TILE, keys:] = jnp.where(seen, 0.0, 1.0).astype(BF16)
            vs[slot, :keys, :DH] = cache_ref[t * keys : (t + 1) * keys, DH:]
            lhs = stacked_queries(q_ref, t * OWN_TILE, 0, OWN_TILE)
            scores = jnp.dot(lhs, kt[slot], preferred_element_type=F32)
            new_max, total = absorb(scores, None, vs[slot])
            start = t * OWN_TILE // TILE * LHS + t * OWN_TILE % TILE
            for g in range(GROUPS):
                rows = slice(start + g * TILE, start + g * TILE + OWN_TILE)
                m_out[rows, :] = new_max[g * OWN_TILE : (g + 1) * OWN_TILE]
                a_out[rows, :] = total[g * OWN_TILE : (g + 1) * OWN_TILE]


def load_keys(parts, kt, vs):
    count = parts[0].shape[0]
    for i, part in enumerate(parts):
        kt[0, :, i * count : (i + 1) * count] = part[:, :DH].T
        vs[i * count : (i + 1) * count, :DH] = part[:, DH:]
    vs[:, DH:] = jnp.ones((len(parts) * count, DH), BF16)


def load_mask(meta, plan, block, pos_ref, kt):
    own = (meta[1] * 4 + meta[2]) * 2
    bound = jnp.where(meta[0] == 1, 1e9, column_of(pos_ref[own + block]))
    pieces = [(dy, dz, flip) for dy, flip in plan for dz in Z_ORDER]
    for j, (dy, dz, flip) in enumerate(pieces):
        source = ((meta[1] - dy) & 3) * 4 + ((meta[2] - dz) & 3)
        key_pos = pos_ref[source * 2 + (meta[0] ^ flip)].astype(F32)
        hidden = jnp.where(key_pos > bound, 1.0, 0.0).astype(BF16)
        kt[1 + block, :, j * HALF : (j + 1) * HALF] = hidden


def prefix_kernel(n_parts, plan, meta, pos_ref, q_ref, *refs):
    parts = refs[:n_parts]
    m_in, a_in, m_out, a_out, kt, vs = refs[n_parts:]
    load_keys(parts, kt, vs)
    for block in range(ROWS // HALF):
        load_mask(meta, plan, block, pos_ref, kt)
    tiles = ROWS // TILE

    def scores_of(t):
        return scores_at(q_ref, kt, t * TILE, t * TILE % HALF, t * TILE // HALF)

    ready = scores_of(0)
    for t in range(tiles):
        following = scores_of(t + 1) if t + 1 < tiles else None
        rows = slice(t * LHS, (t + 1) * LHS)
        new_max, total = fold_in(ready, m_in[rows, :], a_in[rows, :], vs)
        m_out[rows, :] = new_max
        a_out[rows, :] = total
        ready = following


def scores_at(q_ref, kt, first_row, first_col, block):
    lhs = stacked_queries(q_ref, first_row, first_col)
    keys = jnp.concatenate([kt[0], kt[1 + block]], axis=0)
    return jnp.dot(lhs, keys, preferred_element_type=F32)


def fold_in(scores, old_max, old_total, vs):
    new_max, total = absorb(scores, old_max, vs[...])
    factor = jnp.exp2((old_max - new_max) * EXP_SCALE)
    return new_max, old_total * jnp.concatenate([factor, factor], axis=1) + total


def last_kernel(n_parts, plan, places, meta, pos_ref, q_ref, *refs):
    parts = refs[:n_parts]
    m_in, a_in, w_ref = refs[n_parts : n_parts + 3]
    outs = refs[n_parts + 3 : n_parts + 3 + len(places)]
    kt, vs, att = refs[n_parts + 3 + len(places) :]
    cols = w_ref.shape[1] // W_CHUNKS
    load_keys(parts, kt, vs)
    for block in range(ROWS // HALF):
        load_mask(meta, plan, block, pos_ref, kt)
    tiles = HALF // TILE

    def place_of(t):
        dz, dx = places[t]
        return meta[3] ^ dz, (meta[4] + dx) & (tiles - 1)

    def scores_of(t):
        block, tile = place_of(t)
        first_col = pl.multiple_of(tile * TILE, TILE)
        first_row = pl.multiple_of(block * HALF + first_col, TILE)
        return scores_at(q_ref, kt, first_row, first_col, block)

    ready = scores_of(0)
    for t in range(len(places)):
        following = scores_of(t + 1) if t + 1 < len(places) else None
        block, tile = place_of(t)
        rows = pl.ds(pl.multiple_of((block * tiles + tile) * LHS, LHS), LHS)
        _, total = fold_in(ready, m_in[rows, :], a_in[rows, :], vs)
        attended = (total[:, :DH] / total[:, DH:]).astype(BF16)
        for g in range(GROUPS):
            att[t * TILE : (t + 1) * TILE, g * DH : (g + 1) * DH] = attended[
                g * TILE : (g + 1) * TILE
            ]
        ready = following
    for c in range(W_CHUNKS):
        window = slice(c * cols, (c + 1) * cols)
        term = jnp.dot(att[...], w_ref[:, window], preferred_element_type=F32)
        term = term.astype(BF16)
        for t in range(len(places)):
            outs[t][:, window] = term[t * TILE : (t + 1) * TILE]


def params(mebibytes):
    return pltpu.CompilerParams(vmem_limit_bytes=mebibytes * 2**20)


def cost(keys, rows=ROWS, extra=0):
    work = rows * GROUPS * keys
    return pl.CostEstimate(
        flops=8 * DH * work + extra, bytes_accessed=rows * 2**14, transcendentals=work
    )


VMEM = pl.BlockSpec(memory_space=pltpu.VMEM)
SMEM = pl.BlockSpec(memory_space=pltpu.SMEM)
HBM = pl.BlockSpec(memory_space=pltpu.HBM)


def own_call(meta, lengths, q, cache, fresh):
    keys = OWN_TILE // STEPS * CACHE + HALF
    return pl.pallas_call(
        own_kernel,
        in_specs=[SMEM, VMEM, HBM, HBM, HBM],
        out_specs=[VMEM] * 2,
        scratch_shapes=[
            pltpu.VMEM((SLOTS, 2 * DH, keys), BF16),
            pltpu.VMEM((SLOTS, keys, 2 * DH), BF16),
            pltpu.VMEM(q.shape, BF16),
            pltpu.VMEM(cache.shape, BF16),
            pltpu.VMEM(fresh.shape, BF16),
            pltpu.SemaphoreType.DMA((2 + ROWS // OWN_TILE,)),
        ],
        out_shape=[
            jax.ShapeDtypeStruct((ROWS * GROUPS, DH), F32),
            jax.ShapeDtypeStruct((ROWS * GROUPS, 2 * DH), F32),
        ],
        compiler_params=params(50),
        cost_estimate=cost(keys),
        name="own_keys",
    )(meta, lengths, q, cache, fresh)


def prefix_call(name, plan, meta, pos, q, parts, state, rows=ROWS):
    n_parts = len(parts)
    keys = sum(p.shape[0] for p in parts)
    return pl.pallas_call(
        functools.partial(prefix_kernel, n_parts, plan),
        in_specs=[SMEM] + [VMEM] * (4 + n_parts),
        out_specs=[VMEM] * 2,
        scratch_shapes=[
            pltpu.VMEM((1 + ROWS // HALF, DH, keys), BF16),
            pltpu.VMEM((keys, 2 * DH), BF16),
        ],
        out_shape=[jax.ShapeDtypeStruct(s.shape, F32) for s in state],
        input_output_aliases={3 + n_parts: 0, 4 + n_parts: 1},
        compiler_params=params(20),
        cost_estimate=cost(keys, rows),
        name=name,
    )(meta, pos, q, *parts, *state)


def last_call(name, plan, places, meta, pos, q, parts, state, out_weight):
    n_parts = len(parts)
    keys = sum(p.shape[0] for p in parts)
    width = out_weight.shape[1]
    rows = TILE * len(places)
    terms = pl.pallas_call(
        functools.partial(last_kernel, n_parts, plan, places),
        in_specs=[SMEM] + [VMEM] * (5 + n_parts),
        out_specs=[VMEM] * len(places),
        scratch_shapes=[
            pltpu.VMEM((1 + ROWS // HALF, DH, keys), BF16),
            pltpu.VMEM((keys, 2 * DH), BF16),
            pltpu.VMEM((rows, GROUPS * DH), BF16),
        ],
        out_shape=[jax.ShapeDtypeStruct((TILE, width), BF16)] * len(places),
        compiler_params=params(20),
        cost_estimate=cost(keys, rows, 2 * rows * out_weight.size),
        name=name,
    )(meta, pos, q, *parts, *state, out_weight)
    return dict(zip(places, terms))


def on_device(queries, fresh_kv, positions, cache_kv, cache_lengths, out_weight):
    q = queries[0]
    own_kv = fresh_kv[0]
    section = lax.axis_index("section")
    seq = lax.axis_index("seq")
    head = lax.axis_index("head")

    meta = jnp.stack([section, seq >> 2, seq & 3, head >> 2, head & 3])
    pos = positions.reshape(-1, 1, HALF)
    lengths = cache_lengths.reshape(1, HALF)
    cache = cache_kv.reshape(ROWS // STEPS * CACHE, 2 * DH)

    other_kv = lax.ppermute(own_kv, "section", SWAP)
    mine = jnp.where(section == 0, own_kv[:HALF], other_kv[HALF:])
    blocks = [mine] + [lax.ppermute(mine, "seq", seq_perm(0, d)) for d in Z_ORDER[1:]]
    own_inputs = lax.optimization_barrier((mine, meta, lengths, pos))
    _, meta, lengths, pos = own_inputs
    state = own_call(meta, lengths, q, cache, own_kv)
    blocks[3], state = lax.optimization_barrier((blocks[3], state))
    near = jnp.concatenate(blocks, axis=0)
    far = {d: lax.ppermute(near, "seq", seq_perm(d, 0)) for d in (1, 3)}
    near_swapped = lax.ppermute(near, "section", SWAP)
    state = prefix_call("near_keys", NEAR, meta, pos, q, [near, near_swapped], state)
    sent, state = lax.optimization_barrier((near, state))
    far[2] = lax.ppermute(sent, "seq", seq_perm(2, 0))
    far[1], far[3], state = lax.optimization_barrier((far[1], far[3], state))
    swapped = {d: lax.ppermute(far[d], "section", SWAP) for d in (1, 3)}
    state = prefix_call("side_keys", SIDES, meta, pos, q, [far[1], far[3]], state, 1)
    far[2], state = lax.optimization_barrier((far[2], state))
    swapped[2] = lax.ppermute(far[2], "section", SWAP)
    rest = [swapped[1], swapped[3], far[2], swapped[2]]
    rest = (meta, pos, q, rest, state, out_weight)
    terms = last_call("last_keys_a", REST, PLACES_A, *rest)
    terms.update(last_call("last_keys_b", REST, PLACES_B, *rest))

    def move(term, dz, dx):
        return lax.ppermute(term, "head", head_perm(dz, dx))

    crossed = move(terms[1, 2], 1, 0)
    left_mirror = move(terms[1, 1], 0, 1)
    right_mirror = move(terms[1, 3], 0, 3)
    left = move(terms[0, 1], 0, 1)
    right = move(terms[0, 3], 0, 3)
    opposite = move(added(crossed, terms[0, 2]), 0, 2)
    mirror = move(added(left_mirror, right_mirror, terms[1, 0]), 1, 0)
    return added(terms[0, 0], mirror, opposite, left, right)[None]


def added(first, *others):
    total = first.astype(F32)
    for other in others:
        total = total + other.astype(F32)
    return total.astype(BF16)


def solution(mesh):
    in_specs = (
        P("section", "seq", "head"),
        P("section", "seq", "head"),
        P(),
        P("seq", None, "head"),
        P("seq"),
        P("head", None),
    )
    out_specs = P("section", ("seq", "head"), None)
    return jax.shard_map(
        on_device, mesh=mesh, in_specs=in_specs, out_specs=out_specs, check_vma=False
    )
```

```python
import functools
import math

import jax
import jax.numpy as jnp
from jax import lax
from jax.experimental import pallas as pl
from jax.experimental.pallas import tpu as pltpu
from jax.sharding import PartitionSpec as P

HQ = 64
KVH = 8
DH = 128
STEPS = 2
CACHE = 32
GROUPS = HQ // KVH
ROWS = 256
HALF = 128
TILE = 32
OWN_TILE = 16
LHS = TILE * GROUPS
NEG = -1e30
BIG = float(2**22)
EXP_SCALE = DH**-0.5 * math.log2(math.e)
BF16 = jnp.bfloat16
F32 = jnp.float32
Z_ORDER = (0, 2, 1, 3)


W_CHUNKS = 8
SLOTS = 8


def seq_perm(dy, dz):
    return [
        (y * 4 + z, ((y + dy) % 4) * 4 + (z + dz) % 4)
        for y in range(4)
        for z in range(4)
    ]


def head_perm(dz, dx):
    return [
        (z * 4 + x, (z ^ dz) * 4 + (x + dx) % 4)
        for z in range(2)
        for x in range(4)
    ]


SWAP = [(0, 1), (1, 0)]
NEAR = ((0, 0), (0, 1))
SIDES = ((1, 0), (3, 0))
REST = ((1, 1), (3, 1), (2, 0), (2, 1))
PLACES_A = ((1, 2), (1, 1), (1, 3), (0, 1), (0, 3))
PLACES_B = ((0, 2), (1, 0), (0, 0))


def stacked_queries(q_ref, first_row, first_col, tile=TILE):
    stack = jnp.concatenate(
        [q_ref[pl.ds(first_row, tile), g * DH : (g + 1) * DH] for g in range(GROUPS)],
        axis=0,
    )
    rows = lax.broadcasted_iota(jnp.int32, (tile * GROUPS, HALF), 0)
    cols = lax.broadcasted_iota(jnp.int32, (tile * GROUPS, HALF), 1)
    marks = jnp.where((rows & (tile - 1)) + first_col == cols, -BIG, 0.0).astype(BF16)
    return jnp.concatenate([stack, marks], axis=1)


def column_of(row, repeat=1, first=0):
    row = row.astype(F32)
    rows = lax.broadcasted_iota(jnp.int32, (HALF, HALF), 0) // repeat + first
    cols = lax.broadcasted_iota(jnp.int32, (HALF, HALF), 1)
    spread = jnp.where(rows == cols, jnp.broadcast_to(row, (HALF, HALF)), 0.0)
    return jnp.sum(spread, axis=1, keepdims=True)


def absorb(scores, old_max, values):
    width = scores.shape[1]
    top = scores[:, :DH]
    for j in range(DH, width, DH):
        top = jnp.maximum(top, scores[:, j : j + DH])
    new_max = jnp.max(top, axis=1, keepdims=True)
    if old_max is not None:
        new_max = jnp.maximum(old_max, new_max)
    else:
        new_max = jnp.broadcast_to(new_max, (scores.shape[0], DH))
    wide = jnp.concatenate([new_max] * (width // DH), axis=1)
    weights = jnp.exp2((scores - wide) * EXP_SCALE).astype(BF16)
    return new_max, jnp.dot(weights, values, preferred_element_type=F32)


def own_kernel(
    meta, len_ref, q_hbm, cache_hbm, fresh_hbm, m_out, a_out, kt, vs, q_ref, cache_ref, fresh_ref, sems
):
    keys = OWN_TILE // STEPS * CACHE
    tiles = ROWS // OWN_TILE

    @pl.when(meta[0] == 0)
    def _():
        m_out[...] = jnp.full(m_out.shape, NEG, F32)
        a_out[...] = jnp.zeros(a_out.shape, F32)

    @pl.when(meta[0] == 1)
    def _():
        def cache_copy(t):
            window = pl.ds(t * keys, keys)
            return pltpu.make_async_copy(
                cache_hbm.at[window], cache_ref.at[window], sems.at[2 + t]
            )

        fresh_copy = pltpu.make_async_copy(fresh_hbm, fresh_ref, sems.at[0])
        q_copy = pltpu.make_async_copy(q_hbm, q_ref, sems.at[1])
        fresh_copy.start()
        cache_copy(0).start()
        q_copy.start()
        for t in range(1, tiles):
            cache_copy(t).start()
        row = lax.broadcasted_iota(jnp.int32, (OWN_TILE, keys), 0)
        key = lax.broadcasted_iota(jnp.int32, (OWN_TILE, keys), 1)
        same = (key // CACHE) == (row // STEPS)
        nth = (key % CACHE).astype(F32)
        frow = lax.broadcasted_iota(jnp.int32, (OWN_TILE, HALF), 0)
        fkey = lax.broadcasted_iota(jnp.int32, (OWN_TILE, HALF), 1)
        for slot in range(SLOTS):
            kt[slot, DH + OWN_TILE :, :] = jnp.zeros((DH - OWN_TILE, keys + HALF), BF16)
            vs[slot, :, DH:] = jnp.ones((keys + HALF, DH), BF16)
        fresh_copy.wait()
        for t in range(tiles):
            slot = t % SLOTS
            block, mine = t * OWN_TILE // HALF, frow + t * OWN_TILE % HALF
            if t * OWN_TILE % HALF == 0:
                lengths = column_of(len_ref[...], STEPS, block * (HALF // STEPS))
                fresh = slice(block * HALF, (block + 1) * HALF)
                for at in range(SLOTS):
                    kt[at, :DH, keys:] = fresh_ref[fresh, :DH].T
                    vs[at, keys:, :DH] = fresh_ref[fresh, DH:]
            if t == 0:
                q_copy.wait()
            if t % SLOTS == 0:
                for ahead in range(t, t + SLOTS):
                    cache_copy(ahead).wait()
            kt[slot, :DH, :keys] = cache_ref[t * keys : (t + 1) * keys, :DH].T
            first = t * OWN_TILE % HALF
            seen = same & (nth < lengths[first : first + OWN_TILE])
            kt[slot, DH : DH + OWN_TILE, :keys] = jnp.where(seen, 0.0, 1.0).astype(BF16)
            seen = ((mine // STEPS) == (fkey // STEPS)) & (fkey <= mine)
            kt[slot, DH : DH + OWN_TILE, keys:] = jnp.where(seen, 0.0, 1.0).astype(BF16)
            vs[slot, :keys, :DH] = cache_ref[t * keys : (t + 1) * keys, DH:]
            lhs = stacked_queries(q_ref, t * OWN_TILE, 0, OWN_TILE)
            scores = jnp.dot(lhs, kt[slot], preferred_element_type=F32)
            new_max, total = absorb(scores, None, vs[slot])
            start = t * OWN_TILE // TILE * LHS + t * OWN_TILE % TILE
            for g in range(GROUPS):
                rows = slice(start + g * TILE, start + g * TILE + OWN_TILE)
                m_out[rows, :] = new_max[g * OWN_TILE : (g + 1) * OWN_TILE]
                a_out[rows, :] = total[g * OWN_TILE : (g + 1) * OWN_TILE]


def load_keys(parts, kt, vs):
    count = parts[0].shape[0]
    for i, part in enumerate(parts):
        kt[0, :, i * count : (i + 1) * count] = part[:, :DH].T
        vs[i * count : (i + 1) * count, :DH] = part[:, DH:]
    vs[:, DH:] = jnp.ones((len(parts) * count, DH), BF16)


def load_mask(meta, plan, block, pos_ref, kt):
    own = (meta[1] * 4 + meta[2]) * 2
    bound = jnp.where(meta[0] == 1, 1e9, column_of(pos_ref[own + block]))
    pieces = [(dy, dz, flip) for dy, flip in plan for dz in Z_ORDER]
    for j, (dy, dz, flip) in enumerate(pieces):
        source = ((meta[1] - dy) & 3) * 4 + ((meta[2] - dz) & 3)
        key_pos = pos_ref[source * 2 + (meta[0] ^ flip)].astype(F32)
        hidden = jnp.where(key_pos > bound, 1.0, 0.0).astype(BF16)
        kt[1 + block, :, j * HALF : (j + 1) * HALF] = hidden


def prefix_kernel(n_parts, plan, meta, pos_ref, q_ref, *refs):
    parts = refs[:n_parts]
    m_in, a_in, m_out, a_out, kt, vs = refs[n_parts:]
    load_keys(parts, kt, vs)
    for block in range(ROWS // HALF):
        load_mask(meta, plan, block, pos_ref, kt)
    tiles = ROWS // TILE

    def scores_of(t):
        return scores_at(q_ref, kt, t * TILE, t * TILE % HALF, t * TILE // HALF)

    ready = scores_of(0)
    for t in range(tiles):
        following = scores_of(t + 1) if t + 1 < tiles else None
        rows = slice(t * LHS, (t + 1) * LHS)
        new_max, total = fold_in(ready, m_in[rows, :], a_in[rows, :], vs)
        m_out[rows, :] = new_max
        a_out[rows, :] = total
        ready = following


def scores_at(q_ref, kt, first_row, first_col, block):
    lhs = stacked_queries(q_ref, first_row, first_col)
    keys = jnp.concatenate([kt[0], kt[1 + block]], axis=0)
    return jnp.dot(lhs, keys, preferred_element_type=F32)


def fold_in(scores, old_max, old_total, vs):
    new_max, total = absorb(scores, old_max, vs[...])
    factor = jnp.exp2((old_max - new_max) * EXP_SCALE)
    return new_max, old_total * jnp.concatenate([factor, factor], axis=1) + total


def last_kernel(n_parts, plan, places, meta, pos_ref, q_ref, *refs):
    parts = refs[:n_parts]
    m_in, a_in, w_ref = refs[n_parts : n_parts + 3]
    outs = refs[n_parts + 3 : n_parts + 3 + len(places)]
    kt, vs, att = refs[n_parts + 3 + len(places) :]
    cols = w_ref.shape[1] // W_CHUNKS
    load_keys(parts, kt, vs)
    for block in range(ROWS // HALF):
        load_mask(meta, plan, block, pos_ref, kt)
    tiles = HALF // TILE

    def place_of(t):
        dz, dx = places[t]
        return meta[3] ^ dz, (meta[4] + dx) & (tiles - 1)

    def scores_of(t):
        block, tile = place_of(t)
        first_col = pl.multiple_of(tile * TILE, TILE)
        first_row = pl.multiple_of(block * HALF + first_col, TILE)
        return scores_at(q_ref, kt, first_row, first_col, block)

    ready = scores_of(0)
    for t in range(len(places)):
        following = scores_of(t + 1) if t + 1 < len(places) else None
        block, tile = place_of(t)
        rows = pl.ds(pl.multiple_of((block * tiles + tile) * LHS, LHS), LHS)
        _, total = fold_in(ready, m_in[rows, :], a_in[rows, :], vs)
        attended = (total[:, :DH] / total[:, DH:]).astype(BF16)
        for g in range(GROUPS):
            att[t * TILE : (t + 1) * TILE, g * DH : (g + 1) * DH] = attended[
                g * TILE : (g + 1) * TILE
            ]
        ready = following
    for c in range(W_CHUNKS):
        window = slice(c * cols, (c + 1) * cols)
        term = jnp.dot(att[...], w_ref[:, window], preferred_element_type=F32)
        term = term.astype(BF16)
        for t in range(len(places)):
            outs[t][:, window] = term[t * TILE : (t + 1) * TILE]


def params(mebibytes):
    return pltpu.CompilerParams(vmem_limit_bytes=mebibytes * 2**20)


def cost(keys, rows=ROWS, extra=0):
    work = rows * GROUPS * keys
    return pl.CostEstimate(
        flops=8 * DH * work + extra, bytes_accessed=rows * 2**14, transcendentals=work
    )


VMEM = pl.BlockSpec(memory_space=pltpu.VMEM)
SMEM = pl.BlockSpec(memory_space=pltpu.SMEM)
HBM = pl.BlockSpec(memory_space=pltpu.HBM)


def own_call(meta, lengths, q, cache, fresh):
    keys = OWN_TILE // STEPS * CACHE + HALF
    return pl.pallas_call(
        own_kernel,
        in_specs=[SMEM, VMEM, HBM, HBM, HBM],
        out_specs=[VMEM] * 2,
        scratch_shapes=[
            pltpu.VMEM((SLOTS, 2 * DH, keys), BF16),
            pltpu.VMEM((SLOTS, keys, 2 * DH), BF16),
            pltpu.VMEM(q.shape, BF16),
            pltpu.VMEM(cache.shape, BF16),
            pltpu.VMEM(fresh.shape, BF16),
            pltpu.SemaphoreType.DMA((2 + ROWS // OWN_TILE,)),
        ],
        out_shape=[
            jax.ShapeDtypeStruct((ROWS * GROUPS, DH), F32),
            jax.ShapeDtypeStruct((ROWS * GROUPS, 2 * DH), F32),
        ],
        compiler_params=params(50),
        cost_estimate=cost(keys),
        name="own_keys",
    )(meta, lengths, q, cache, fresh)


def prefix_call(name, plan, meta, pos, q, parts, state, rows=ROWS):
    n_parts = len(parts)
    keys = sum(p.shape[0] for p in parts)
    return pl.pallas_call(
        functools.partial(prefix_kernel, n_parts, plan),
        in_specs=[SMEM] + [VMEM] * (4 + n_parts),
        out_specs=[VMEM] * 2,
        scratch_shapes=[
            pltpu.VMEM((1 + ROWS // HALF, DH, keys), BF16),
            pltpu.VMEM((keys, 2 * DH), BF16),
        ],
        out_shape=[jax.ShapeDtypeStruct(s.shape, F32) for s in state],
        input_output_aliases={3 + n_parts: 0, 4 + n_parts: 1},
        compiler_params=params(20),
        cost_estimate=cost(keys, rows),
        name=name,
    )(meta, pos, q, *parts, *state)


def last_call(name, plan, places, meta, pos, q, parts, state, out_weight):
    n_parts = len(parts)
    keys = sum(p.shape[0] for p in parts)
    width = out_weight.shape[1]
    rows = TILE * len(places)
    terms = pl.pallas_call(
        functools.partial(last_kernel, n_parts, plan, places),
        in_specs=[SMEM] + [VMEM] * (5 + n_parts),
        out_specs=[VMEM] * len(places),
        scratch_shapes=[
            pltpu.VMEM((1 + ROWS // HALF, DH, keys), BF16),
            pltpu.VMEM((keys, 2 * DH), BF16),
            pltpu.VMEM((rows, GROUPS * DH), BF16),
        ],
        out_shape=[jax.ShapeDtypeStruct((TILE, width), BF16)] * len(places),
        compiler_params=params(20),
        cost_estimate=cost(keys, rows, 2 * rows * out_weight.size),
        name=name,
    )(meta, pos, q, *parts, *state, out_weight)
    return dict(zip(places, terms))


def on_device(queries, fresh_kv, positions, cache_kv, cache_lengths, out_weight):
    q = queries[0]
    own_kv = fresh_kv[0]
    section = lax.axis_index("section")
    seq = lax.axis_index("seq")
    head = lax.axis_index("head")

    meta = jnp.stack([section, seq >> 2, seq & 3, head >> 2, head & 3])
    pos = positions.reshape(-1, 1, HALF)
    lengths = cache_lengths.reshape(1, HALF)
    cache = cache_kv.reshape(ROWS // STEPS * CACHE, 2 * DH)

    other_kv = lax.ppermute(own_kv, "section", SWAP)
    mine = jnp.where(section == 0, own_kv[:HALF], other_kv[HALF:])
    blocks = [mine] + [lax.ppermute(mine, "seq", seq_perm(0, d)) for d in Z_ORDER[1:]]
    own_inputs = lax.optimization_barrier((mine, meta, lengths, pos))
    _, meta, lengths, pos = own_inputs
    state = own_call(meta, lengths, q, cache, own_kv)
    blocks[3], state = lax.optimization_barrier((blocks[3], state))
    near = jnp.concatenate(blocks, axis=0)
    far = {d: lax.ppermute(near, "seq", seq_perm(d, 0)) for d in (1, 3)}
    near_swapped = lax.ppermute(near, "section", SWAP)
    state = prefix_call("near_keys", NEAR, meta, pos, q, [near, near_swapped], state)
    sent, far[1], far[3], state = lax.optimization_barrier((near, far[1], far[3], state))
    far[2] = lax.ppermute(sent, "seq", seq_perm(2, 0))
    swapped = {d: lax.ppermute(far[d], "section", SWAP) for d in (1, 3)}
    state = prefix_call("side_keys", SIDES, meta, pos, q, [far[1], far[3]], state, 1)
    far[2], state = lax.optimization_barrier((far[2], state))
    swapped[2] = lax.ppermute(far[2], "section", SWAP)
    rest = [swapped[1], swapped[3], far[2], swapped[2]]
    rest = (meta, pos, q, rest, state, out_weight)
    terms = last_call("last_keys_a", REST, PLACES_A, *rest)
    terms.update(last_call("last_keys_b", REST, PLACES_B, *rest))

    def move(term, dz, dx):
        return lax.ppermute(term, "head", head_perm(dz, dx))

    crossed = move(terms[1, 2], 1, 0)
    left_mirror = move(terms[1, 1], 0, 1)
    right_mirror = move(terms[1, 3], 0, 3)
    left = move(terms[0, 1], 0, 1)
    right = move(terms[0, 3], 0, 3)
    opposite = move(added(crossed, terms[0, 2]), 0, 2)
    mirror = move(added(left_mirror, right_mirror, terms[1, 0]), 1, 0)
    return added(terms[0, 0], mirror, opposite, left, right)[None]


def added(first, *others):
    total = first.astype(F32)
    for other in others:
        total = total + other.astype(F32)
    return total.astype(BF16)


def solution(mesh):
    in_specs = (
        P("section", "seq", "head"),
        P("section", "seq", "head"),
        P(),
        P("seq", None, "head"),
        P("seq"),
        P("head", None),
    )
    out_specs = P("section", ("seq", "head"), None)
    return jax.shard_map(
        on_device, mesh=mesh, in_specs=in_specs, out_specs=out_specs, check_vma=False
    )
```

```python
import functools
import math

import jax
import jax.numpy as jnp
from jax import lax
from jax.experimental import pallas as pl
from jax.experimental.pallas import tpu as pltpu
from jax.sharding import PartitionSpec as P

HQ = 64
KVH = 8
DH = 128
STEPS = 2
CACHE = 32
GROUPS = HQ // KVH
ROWS = 256
HALF = 128
TILE = 32
OWN_TILE = 16
LHS = TILE * GROUPS
NEG = -1e30
BIG = float(2**22)
EXP_SCALE = DH**-0.5 * math.log2(math.e)
BF16 = jnp.bfloat16
F32 = jnp.float32
Z_ORDER = (0, 2, 1, 3)


W_CHUNKS = 8
SLOTS = 8


def seq_perm(dy, dz):
    return [
        (y * 4 + z, ((y + dy) % 4) * 4 + (z + dz) % 4)
        for y in range(4)
        for z in range(4)
    ]


def both_sides():
    return [
        (16 * section + i, 16 * section + j)
        for section, dy in enumerate((1, 3))
        for i, j in seq_perm(dy, 0)
    ]


def head_perm(dz, dx):
    return [
        (z * 4 + x, (z ^ dz) * 4 + (x + dx) % 4)
        for z in range(2)
        for x in range(4)
    ]


SWAP = [(0, 1), (1, 0)]
NEAR = ((0, 0, 0), (0, 0, 1))
BESIDE = ((1, 2, 0), (1, 2, 1))
REST = ((3, -2, 1), (3, -2, 0), (2, 0, 0), (2, 0, 1))
PLACES_A = ((1, 2), (1, 1), (1, 3), (0, 1), (0, 3))
PLACES_B = ((0, 2), (1, 0), (0, 0))


def stacked_queries(q_ref, first_row, first_col, tile=TILE):
    stack = jnp.concatenate(
        [q_ref[pl.ds(first_row, tile), g * DH : (g + 1) * DH] for g in range(GROUPS)],
        axis=0,
    )
    rows = lax.broadcasted_iota(jnp.int32, (tile * GROUPS, HALF), 0)
    cols = lax.broadcasted_iota(jnp.int32, (tile * GROUPS, HALF), 1)
    marks = jnp.where((rows & (tile - 1)) + first_col == cols, -BIG, 0.0).astype(BF16)
    return jnp.concatenate([stack, marks], axis=1)


def column_of(row, repeat=1, first=0):
    row = row.astype(F32)
    rows = lax.broadcasted_iota(jnp.int32, (HALF, HALF), 0) // repeat + first
    cols = lax.broadcasted_iota(jnp.int32, (HALF, HALF), 1)
    spread = jnp.where(rows == cols, jnp.broadcast_to(row, (HALF, HALF)), 0.0)
    return jnp.sum(spread, axis=1, keepdims=True)


def absorb(scores, old_max, values):
    width = scores.shape[1]
    top = scores[:, :DH]
    for j in range(DH, width, DH):
        top = jnp.maximum(top, scores[:, j : j + DH])
    new_max = jnp.max(top, axis=1, keepdims=True)
    if old_max is not None:
        new_max = jnp.maximum(old_max, new_max)
    else:
        new_max = jnp.broadcast_to(new_max, (scores.shape[0], DH))
    wide = jnp.concatenate([new_max] * (width // DH), axis=1)
    weights = jnp.exp2((scores - wide) * EXP_SCALE).astype(BF16)
    return new_max, jnp.dot(weights, values, preferred_element_type=F32)


def own_kernel(
    meta, len_ref, q_hbm, cache_hbm, fresh_hbm, m_out, a_out, kt, vs, q_ref, cache_ref, fresh_ref, sems
):
    keys = OWN_TILE // STEPS * CACHE
    tiles = ROWS // OWN_TILE

    @pl.when(meta[0] == 0)
    def _():
        m_out[...] = jnp.full(m_out.shape, NEG, F32)
        a_out[...] = jnp.zeros(a_out.shape, F32)

    @pl.when(meta[0] == 1)
    def _():
        def cache_copy(t):
            window = pl.ds(t * keys, keys)
            return pltpu.make_async_copy(
                cache_hbm.at[window], cache_ref.at[window], sems.at[2 + t]
            )

        fresh_copy = pltpu.make_async_copy(fresh_hbm, fresh_ref, sems.at[0])
        q_copy = pltpu.make_async_copy(q_hbm, q_ref, sems.at[1])
        fresh_copy.start()
        cache_copy(0).start()
        q_copy.start()
        for t in range(1, tiles):
            cache_copy(t).start()
        row = lax.broadcasted_iota(jnp.int32, (OWN_TILE, keys), 0)
        key = lax.broadcasted_iota(jnp.int32, (OWN_TILE, keys), 1)
        same = (key // CACHE) == (row // STEPS)
        nth = (key % CACHE).astype(F32)
        frow = lax.broadcasted_iota(jnp.int32, (OWN_TILE, HALF), 0)
        fkey = lax.broadcasted_iota(jnp.int32, (OWN_TILE, HALF), 1)
        for slot in range(SLOTS):
            kt[slot, DH + OWN_TILE :, :] = jnp.zeros((DH - OWN_TILE, keys + HALF), BF16)
            vs[slot, :, DH:] = jnp.ones((keys + HALF, DH), BF16)
        fresh_copy.wait()
        for t in range(tiles):
            slot = t % SLOTS
            block, mine = t * OWN_TILE // HALF, frow + t * OWN_TILE % HALF
            if t * OWN_TILE % HALF == 0:
                lengths = column_of(len_ref[...], STEPS, block * (HALF // STEPS))
                fresh = slice(block * HALF, (block + 1) * HALF)
                for at in range(SLOTS):
                    kt[at, :DH, keys:] = fresh_ref[fresh, :DH].T
                    vs[at, keys:, :DH] = fresh_ref[fresh, DH:]
            if t == 0:
                q_copy.wait()
            if t % SLOTS == 0:
                for ahead in range(t, t + SLOTS):
                    cache_copy(ahead).wait()
            kt[slot, :DH, :keys] = cache_ref[t * keys : (t + 1) * keys, :DH].T
            first = t * OWN_TILE % HALF
            seen = same & (nth < lengths[first : first + OWN_TILE])
            kt[slot, DH : DH + OWN_TILE, :keys] = jnp.where(seen, 0.0, 1.0).astype(BF16)
            seen = ((mine // STEPS) == (fkey // STEPS)) & (fkey <= mine)
            kt[slot, DH : DH + OWN_TILE, keys:] = jnp.where(seen, 0.0, 1.0).astype(BF16)
            vs[slot, :keys, :DH] = cache_ref[t * keys : (t + 1) * keys, DH:]
            lhs = stacked_queries(q_ref, t * OWN_TILE, 0, OWN_TILE)
            scores = jnp.dot(lhs, kt[slot], preferred_element_type=F32)
            new_max, total = absorb(scores, None, vs[slot])
            start = t * OWN_TILE // TILE * LHS + t * OWN_TILE % TILE
            for g in range(GROUPS):
                rows = slice(start + g * TILE, start + g * TILE + OWN_TILE)
                m_out[rows, :] = new_max[g * OWN_TILE : (g + 1) * OWN_TILE]
                a_out[rows, :] = total[g * OWN_TILE : (g + 1) * OWN_TILE]


def load_keys(parts, kt, vs):
    first = 0
    for part in parts:
        rows = slice(first, first + part.shape[0])
        kt[0, :, rows] = part[:, :DH].T
        vs[rows, :DH] = part[:, DH:]
        first = rows.stop
    vs[:, DH:] = jnp.ones((first, DH), BF16)


def load_mask(meta, plan, block, pos_ref, kt):
    own = (meta[1] * 4 + meta[2]) * 2
    bound = jnp.where(meta[0] == 1, 1e9, column_of(pos_ref[own + block]))
    pieces = [half + (dz,) for half in plan for dz in Z_ORDER]
    for j, (dy, change, flip, dz) in enumerate(pieces):
        source = ((meta[1] - dy - change * meta[0]) & 3) * 4 + ((meta[2] - dz) & 3)
        key_pos = pos_ref[source * 2 + (meta[0] ^ flip)].astype(F32)
        hidden = jnp.where(key_pos > bound, 1.0, 0.0).astype(BF16)
        kt[1 + block, :, j * HALF : (j + 1) * HALF] = hidden


def prefix_kernel(n_parts, plan, meta, pos_ref, q_ref, *refs):
    parts = refs[:n_parts]
    m_in, a_in, m_out, a_out, kt, vs = refs[n_parts:]
    load_keys(parts, kt, vs)
    for block in range(ROWS // HALF):
        load_mask(meta, plan, block, pos_ref, kt)
    tiles = ROWS // TILE

    def scores_of(t):
        return scores_at(q_ref, kt, t * TILE, t * TILE % HALF, t * TILE // HALF)

    ready = scores_of(0)
    for t in range(tiles):
        following = scores_of(t + 1) if t + 1 < tiles else None
        rows = slice(t * LHS, (t + 1) * LHS)
        new_max, total = fold_in(ready, m_in[rows, :], a_in[rows, :], vs)
        m_out[rows, :] = new_max
        a_out[rows, :] = total
        ready = following


def scores_at(q_ref, kt, first_row, first_col, block):
    lhs = stacked_queries(q_ref, first_row, first_col)
    keys = jnp.concatenate([kt[0], kt[1 + block]], axis=0)
    return jnp.dot(lhs, keys, preferred_element_type=F32)


def fold_in(scores, old_max, old_total, vs):
    new_max, total = absorb(scores, old_max, vs[...])
    factor = jnp.exp2((old_max - new_max) * EXP_SCALE)
    return new_max, old_total * jnp.concatenate([factor, factor], axis=1) + total


def last_kernel(n_parts, plan, places, meta, pos_ref, q_ref, *refs):
    parts = refs[:n_parts]
    m_in, a_in, w_ref = refs[n_parts : n_parts + 3]
    outs = refs[n_parts + 3 : n_parts + 3 + len(places)]
    kt, vs, att = refs[n_parts + 3 + len(places) :]
    cols = w_ref.shape[1] // W_CHUNKS
    load_keys(parts, kt, vs)
    for block in range(ROWS // HALF):
        load_mask(meta, plan, block, pos_ref, kt)
    tiles = HALF // TILE

    def place_of(t):
        dz, dx = places[t]
        return meta[3] ^ dz, (meta[4] + dx) & (tiles - 1)

    def scores_of(t):
        block, tile = place_of(t)
        first_col = pl.multiple_of(tile * TILE, TILE)
        first_row = pl.multiple_of(block * HALF + first_col, TILE)
        return scores_at(q_ref, kt, first_row, first_col, block)

    ready = scores_of(0)
    for t in range(len(places)):
        following = scores_of(t + 1) if t + 1 < len(places) else None
        block, tile = place_of(t)
        rows = pl.ds(pl.multiple_of((block * tiles + tile) * LHS, LHS), LHS)
        _, total = fold_in(ready, m_in[rows, :], a_in[rows, :], vs)
        attended = (total[:, :DH] / total[:, DH:]).astype(BF16)
        for g in range(GROUPS):
            att[t * TILE : (t + 1) * TILE, g * DH : (g + 1) * DH] = attended[
                g * TILE : (g + 1) * TILE
            ]
        ready = following
    for c in range(W_CHUNKS):
        window = slice(c * cols, (c + 1) * cols)
        term = jnp.dot(att[...], w_ref[:, window], preferred_element_type=F32)
        term = term.astype(BF16)
        for t in range(len(places)):
            outs[t][:, window] = term[t * TILE : (t + 1) * TILE]


def params(mebibytes):
    return pltpu.CompilerParams(vmem_limit_bytes=mebibytes * 2**20)


def cost(keys, rows=ROWS, extra=0):
    work = rows * GROUPS * keys
    return pl.CostEstimate(
        flops=8 * DH * work + extra, bytes_accessed=rows * 2**14, transcendentals=work
    )


VMEM = pl.BlockSpec(memory_space=pltpu.VMEM)
SMEM = pl.BlockSpec(memory_space=pltpu.SMEM)
HBM = pl.BlockSpec(memory_space=pltpu.HBM)


def own_call(meta, lengths, q, cache, fresh):
    keys = OWN_TILE // STEPS * CACHE + HALF
    return pl.pallas_call(
        own_kernel,
        in_specs=[SMEM, VMEM, HBM, HBM, HBM],
        out_specs=[VMEM] * 2,
        scratch_shapes=[
            pltpu.VMEM((SLOTS, 2 * DH, keys), BF16),
            pltpu.VMEM((SLOTS, keys, 2 * DH), BF16),
            pltpu.VMEM(q.shape, BF16),
            pltpu.VMEM(cache.shape, BF16),
            pltpu.VMEM(fresh.shape, BF16),
            pltpu.SemaphoreType.DMA((2 + ROWS // OWN_TILE,)),
        ],
        out_shape=[
            jax.ShapeDtypeStruct((ROWS * GROUPS, DH), F32),
            jax.ShapeDtypeStruct((ROWS * GROUPS, 2 * DH), F32),
        ],
        compiler_params=params(50),
        cost_estimate=cost(keys),
        name="own_keys",
    )(meta, lengths, q, cache, fresh)


def prefix_call(name, plan, meta, pos, q, parts, state, rows=ROWS):
    n_parts = len(parts)
    keys = sum(p.shape[0] for p in parts)
    return pl.pallas_call(
        functools.partial(prefix_kernel, n_parts, plan),
        in_specs=[SMEM] + [VMEM] * (4 + n_parts),
        out_specs=[VMEM] * 2,
        scratch_shapes=[
            pltpu.VMEM((1 + ROWS // HALF, DH, keys), BF16),
            pltpu.VMEM((keys, 2 * DH), BF16),
        ],
        out_shape=[jax.ShapeDtypeStruct(s.shape, F32) for s in state],
        input_output_aliases={3 + n_parts: 0, 4 + n_parts: 1},
        compiler_params=params(20),
        cost_estimate=cost(keys, rows),
        name=name,
    )(meta, pos, q, *parts, *state)


def last_call(name, plan, places, meta, pos, q, parts, state, out_weight):
    n_parts = len(parts)
    keys = sum(p.shape[0] for p in parts)
    width = out_weight.shape[1]
    rows = TILE * len(places)
    terms = pl.pallas_call(
        functools.partial(last_kernel, n_parts, plan, places),
        in_specs=[SMEM] + [VMEM] * (5 + n_parts),
        out_specs=[VMEM] * len(places),
        scratch_shapes=[
            pltpu.VMEM((1 + ROWS // HALF, DH, keys), BF16),
            pltpu.VMEM((keys, 2 * DH), BF16),
            pltpu.VMEM((rows, GROUPS * DH), BF16),
        ],
        out_shape=[jax.ShapeDtypeStruct((TILE, width), BF16)] * len(places),
        compiler_params=params(20),
        cost_estimate=cost(keys, rows, 2 * rows * out_weight.size),
        name=name,
    )(meta, pos, q, *parts, *state, out_weight)
    return dict(zip(places, terms))


def on_device(queries, fresh_kv, positions, cache_kv, cache_lengths, out_weight):
    q = queries[0]
    own_kv = fresh_kv[0]
    section = lax.axis_index("section")
    seq = lax.axis_index("seq")
    head = lax.axis_index("head")

    meta = jnp.stack([section, seq >> 2, seq & 3, head >> 2, head & 3])
    pos = positions.reshape(-1, 1, HALF)
    lengths = cache_lengths.reshape(1, HALF)
    cache = cache_kv.reshape(ROWS // STEPS * CACHE, 2 * DH)

    other_kv = lax.ppermute(own_kv, "section", SWAP)
    mine = jnp.where(section == 0, own_kv[:HALF], other_kv[HALF:])
    blocks = [mine] + [lax.ppermute(mine, "seq", seq_perm(0, d)) for d in Z_ORDER[1:]]
    own_inputs = lax.optimization_barrier((mine, meta, lengths, pos))
    _, meta, lengths, pos = own_inputs
    state = own_call(meta, lengths, q, cache, own_kv)
    blocks[3], state = lax.optimization_barrier((blocks[3], state))
    near = jnp.concatenate(blocks, axis=0)
    near_swapped = lax.ppermute(near, "section", SWAP)
    full = jnp.concatenate([near, near_swapped], axis=0)
    beside = lax.ppermute(full, ("section", "seq"), both_sides())
    state = prefix_call("near_keys", NEAR, meta, pos, q, [near, near_swapped], state)
    sent, beside, state = lax.optimization_barrier((near, beside, state))
    across = lax.ppermute(sent, "seq", seq_perm(2, 0))
    beside_swapped = lax.ppermute(beside, "section", SWAP)
    state = prefix_call("side_keys", BESIDE, meta, pos, q, [beside], state)
    across, state = lax.optimization_barrier((across, state))
    across_swapped = lax.ppermute(across, "section", SWAP)
    rest = [beside_swapped, across, across_swapped]
    rest = (meta, pos, q, rest, state, out_weight)
    terms = last_call("last_keys_a", REST, PLACES_A, *rest)
    terms.update(last_call("last_keys_b", REST, PLACES_B, *rest))

    def move(term, dz, dx):
        return lax.ppermute(term, "head", head_perm(dz, dx))

    crossed = move(terms[1, 2], 1, 0)
    left_mirror = move(terms[1, 1], 0, 1)
    right_mirror = move(terms[1, 3], 0, 3)
    left = move(terms[0, 1], 0, 1)
    right = move(terms[0, 3], 0, 3)
    opposite = move(added(crossed, terms[0, 2]), 0, 2)
    mirror = move(added(left_mirror, right_mirror, terms[1, 0]), 1, 0)
    return added(terms[0, 0], mirror, opposite, left, right)[None]


def added(first, *others):
    total = first.astype(F32)
    for other in others:
        total = total + other.astype(F32)
    return total.astype(BF16)


def solution(mesh):
    in_specs = (
        P("section", "seq", "head"),
        P("section", "seq", "head"),
        P(),
        P("seq", None, "head"),
        P("seq"),
        P("head", None),
    )
    out_specs = P("section", ("seq", "head"), None)
    return jax.shard_map(
        on_device, mesh=mesh, in_specs=in_specs, out_specs=out_specs, check_vma=False
    )
```

```python
import functools
import math

import jax
import jax.numpy as jnp
from jax import lax
from jax.experimental import pallas as pl
from jax.experimental.pallas import tpu as pltpu
from jax.sharding import PartitionSpec as P

HQ = 64
KVH = 8
DH = 128
STEPS = 2
CACHE = 32
GROUPS = HQ // KVH
ROWS = 256
HALF = 128
TILE = 32
OWN_TILE = 16
LHS = TILE * GROUPS
NEG = -1e30
BIG = float(2**22)
EXP_SCALE = DH**-0.5 * math.log2(math.e)
BF16 = jnp.bfloat16
F32 = jnp.float32
Z_ORDER = (0, 2, 1, 3)


W_CHUNKS = 8
SLOTS = 8


def seq_perm(dy, dz):
    return [
        (y * 4 + z, ((y + dy) % 4) * 4 + (z + dz) % 4)
        for y in range(4)
        for z in range(4)
    ]


def head_perm(dz, dx):
    return [
        (z * 4 + x, (z ^ dz) * 4 + (x + dx) % 4)
        for z in range(2)
        for x in range(4)
    ]


SWAP = [(0, 1), (1, 0)]
NEAR = ((0, 0), (0, 1))
SIDES = ((3, 0), (1, 0))
REST = ((3, 1), (1, 1), (2, 0), (2, 1))
PLACES_A = ((1, 2), (1, 1), (1, 3), (0, 1), (0, 3))
PLACES_B = ((0, 2), (1, 0), (0, 0))


def stacked_queries(q_ref, first_row, first_col, tile=TILE):
    stack = jnp.concatenate(
        [q_ref[pl.ds(first_row, tile), g * DH : (g + 1) * DH] for g in range(GROUPS)],
        axis=0,
    )
    rows = lax.broadcasted_iota(jnp.int32, (tile * GROUPS, HALF), 0)
    cols = lax.broadcasted_iota(jnp.int32, (tile * GROUPS, HALF), 1)
    marks = jnp.where((rows & (tile - 1)) + first_col == cols, -BIG, 0.0).astype(BF16)
    return jnp.concatenate([stack, marks], axis=1)


def column_of(row, repeat=1, first=0):
    row = row.astype(F32)
    rows = lax.broadcasted_iota(jnp.int32, (HALF, HALF), 0) // repeat + first
    cols = lax.broadcasted_iota(jnp.int32, (HALF, HALF), 1)
    spread = jnp.where(rows == cols, jnp.broadcast_to(row, (HALF, HALF)), 0.0)
    return jnp.sum(spread, axis=1, keepdims=True)


def absorb(scores, old_max, values):
    width = scores.shape[1]
    top = scores[:, :DH]
    for j in range(DH, width, DH):
        top = jnp.maximum(top, scores[:, j : j + DH])
    new_max = jnp.max(top, axis=1, keepdims=True)
    if old_max is not None:
        new_max = jnp.maximum(old_max, new_max)
    else:
        new_max = jnp.broadcast_to(new_max, (scores.shape[0], DH))
    wide = jnp.concatenate([new_max] * (width // DH), axis=1)
    weights = jnp.exp2((scores - wide) * EXP_SCALE).astype(BF16)
    return new_max, jnp.dot(weights, values, preferred_element_type=F32)


def own_kernel(
    meta, len_ref, q_hbm, cache_hbm, fresh_hbm, m_out, a_out, kt, vs, q_ref, cache_ref, fresh_ref, sems
):
    keys = OWN_TILE // STEPS * CACHE
    tiles = ROWS // OWN_TILE

    @pl.when(meta[0] == 0)
    def _():
        m_out[...] = jnp.full(m_out.shape, NEG, F32)
        a_out[...] = jnp.zeros(a_out.shape, F32)

    @pl.when(meta[0] == 1)
    def _():
        def cache_copy(t):
            window = pl.ds(t * keys, keys)
            return pltpu.make_async_copy(
                cache_hbm.at[window], cache_ref.at[window], sems.at[2 + t]
            )

        fresh_copy = pltpu.make_async_copy(fresh_hbm, fresh_ref, sems.at[0])
        q_copy = pltpu.make_async_copy(q_hbm, q_ref, sems.at[1])
        fresh_copy.start()
        cache_copy(0).start()
        q_copy.start()
        for t in range(1, tiles):
            cache_copy(t).start()
        row = lax.broadcasted_iota(jnp.int32, (OWN_TILE, keys), 0)
        key = lax.broadcasted_iota(jnp.int32, (OWN_TILE, keys), 1)
        same = (key // CACHE) == (row // STEPS)
        nth = (key % CACHE).astype(F32)
        frow = lax.broadcasted_iota(jnp.int32, (OWN_TILE, HALF), 0)
        fkey = lax.broadcasted_iota(jnp.int32, (OWN_TILE, HALF), 1)
        for slot in range(SLOTS):
            kt[slot, DH + OWN_TILE :, :] = jnp.zeros((DH - OWN_TILE, keys + HALF), BF16)
            vs[slot, :, DH:] = jnp.ones((keys + HALF, DH), BF16)
        fresh_copy.wait()
        for t in range(tiles):
            slot = t % SLOTS
            block, mine = t * OWN_TILE // HALF, frow + t * OWN_TILE % HALF
            if t * OWN_TILE % HALF == 0:
                lengths = column_of(len_ref[...], STEPS, block * (HALF // STEPS))
                fresh = slice(block * HALF, (block + 1) * HALF)
                for at in range(SLOTS):
                    kt[at, :DH, keys:] = fresh_ref[fresh, :DH].T
                    vs[at, keys:, :DH] = fresh_ref[fresh, DH:]
            if t == 0:
                q_copy.wait()
            if t % SLOTS == 0:
                for ahead in range(t, t + SLOTS):
                    cache_copy(ahead).wait()
            kt[slot, :DH, :keys] = cache_ref[t * keys : (t + 1) * keys, :DH].T
            first = t * OWN_TILE % HALF
            seen = same & (nth < lengths[first : first + OWN_TILE])
            kt[slot, DH : DH + OWN_TILE, :keys] = jnp.where(seen, 0.0, 1.0).astype(BF16)
            seen = ((mine // STEPS) == (fkey // STEPS)) & (fkey <= mine)
            kt[slot, DH : DH + OWN_TILE, keys:] = jnp.where(seen, 0.0, 1.0).astype(BF16)
            vs[slot, :keys, :DH] = cache_ref[t * keys : (t + 1) * keys, DH:]
            lhs = stacked_queries(q_ref, t * OWN_TILE, 0, OWN_TILE)
            scores = jnp.dot(lhs, kt[slot], preferred_element_type=F32)
            new_max, total = absorb(scores, None, vs[slot])
            start = t * OWN_TILE // TILE * LHS + t * OWN_TILE % TILE
            for g in range(GROUPS):
                rows = slice(start + g * TILE, start + g * TILE + OWN_TILE)
                m_out[rows, :] = new_max[g * OWN_TILE : (g + 1) * OWN_TILE]
                a_out[rows, :] = total[g * OWN_TILE : (g + 1) * OWN_TILE]


def load_keys(parts, kt, vs):
    count = parts[0].shape[0]
    for i, part in enumerate(parts):
        kt[0, :, i * count : (i + 1) * count] = part[:, :DH].T
        vs[i * count : (i + 1) * count, :DH] = part[:, DH:]
    vs[:, DH:] = jnp.ones((len(parts) * count, DH), BF16)


def load_mask(meta, plan, block, pos_ref, kt):
    own = (meta[1] * 4 + meta[2]) * 2
    bound = jnp.where(meta[0] == 1, 1e9, column_of(pos_ref[own + block]))
    pieces = [(dy, dz, flip) for dy, flip in plan for dz in Z_ORDER]
    for j, (dy, dz, flip) in enumerate(pieces):
        source = ((meta[1] - dy) & 3) * 4 + ((meta[2] - dz) & 3)
        key_pos = pos_ref[source * 2 + (meta[0] ^ flip)].astype(F32)
        hidden = jnp.where(key_pos > bound, 1.0, 0.0).astype(BF16)
        kt[1 + block, :, j * HALF : (j + 1) * HALF] = hidden


def prefix_kernel(n_parts, plan, meta, pos_ref, q_ref, *refs):
    parts = refs[:n_parts]
    m_in, a_in, m_out, a_out, kt, vs = refs[n_parts:]
    load_keys(parts, kt, vs)
    for block in range(ROWS // HALF):
        load_mask(meta, plan, block, pos_ref, kt)
    tiles = ROWS // TILE

    def scores_of(t):
        return scores_at(q_ref, kt, t * TILE, t * TILE % HALF, t * TILE // HALF)

    ready = scores_of(0)
    for t in range(tiles):
        following = scores_of(t + 1) if t + 1 < tiles else None
        rows = slice(t * LHS, (t + 1) * LHS)
        new_max, total = fold_in(ready, m_in[rows, :], a_in[rows, :], vs)
        m_out[rows, :] = new_max
        a_out[rows, :] = total
        ready = following


def scores_at(q_ref, kt, first_row, first_col, block):
    lhs = stacked_queries(q_ref, first_row, first_col)
    keys = jnp.concatenate([kt[0], kt[1 + block]], axis=0)
    return jnp.dot(lhs, keys, preferred_element_type=F32)


def fold_in(scores, old_max, old_total, vs):
    new_max, total = absorb(scores, old_max, vs[...])
    factor = jnp.exp2((old_max - new_max) * EXP_SCALE)
    return new_max, old_total * jnp.concatenate([factor, factor], axis=1) + total


def last_kernel(n_parts, plan, places, meta, pos_ref, q_ref, *refs):
    parts = refs[:n_parts]
    m_in, a_in, w_ref = refs[n_parts : n_parts + 3]
    outs = refs[n_parts + 3 : n_parts + 3 + len(places)]
    kt, vs, att = refs[n_parts + 3 + len(places) :]
    cols = w_ref.shape[1] // W_CHUNKS
    load_keys(parts, kt, vs)
    for block in range(ROWS // HALF):
        load_mask(meta, plan, block, pos_ref, kt)
    tiles = HALF // TILE

    def place_of(t):
        dz, dx = places[t]
        return meta[3] ^ dz, (meta[4] + dx) & (tiles - 1)

    def scores_of(t):
        block, tile = place_of(t)
        first_col = pl.multiple_of(tile * TILE, TILE)
        first_row = pl.multiple_of(block * HALF + first_col, TILE)
        return scores_at(q_ref, kt, first_row, first_col, block)

    ready = scores_of(0)
    for t in range(len(places)):
        following = scores_of(t + 1) if t + 1 < len(places) else None
        block, tile = place_of(t)
        rows = pl.ds(pl.multiple_of((block * tiles + tile) * LHS, LHS), LHS)
        _, total = fold_in(ready, m_in[rows, :], a_in[rows, :], vs)
        attended = (total[:, :DH] / total[:, DH:]).astype(BF16)
        for g in range(GROUPS):
            att[t * TILE : (t + 1) * TILE, g * DH : (g + 1) * DH] = attended[
                g * TILE : (g + 1) * TILE
            ]
        ready = following
    for c in range(W_CHUNKS):
        window = slice(c * cols, (c + 1) * cols)
        term = jnp.dot(att[...], w_ref[:, window], preferred_element_type=F32)
        term = term.astype(BF16)
        for t in range(len(places)):
            outs[t][:, window] = term[t * TILE : (t + 1) * TILE]


def params(mebibytes):
    return pltpu.CompilerParams(vmem_limit_bytes=mebibytes * 2**20)


def cost(keys, rows=ROWS, extra=0):
    work = rows * GROUPS * keys
    return pl.CostEstimate(
        flops=8 * DH * work + extra, bytes_accessed=rows * 2**14, transcendentals=work
    )


VMEM = pl.BlockSpec(memory_space=pltpu.VMEM)
SMEM = pl.BlockSpec(memory_space=pltpu.SMEM)
HBM = pl.BlockSpec(memory_space=pltpu.HBM)


def own_call(meta, lengths, q, cache, fresh):
    keys = OWN_TILE // STEPS * CACHE + HALF
    return pl.pallas_call(
        own_kernel,
        in_specs=[SMEM, VMEM, HBM, HBM, HBM],
        out_specs=[VMEM] * 2,
        scratch_shapes=[
            pltpu.VMEM((SLOTS, 2 * DH, keys), BF16),
            pltpu.VMEM((SLOTS, keys, 2 * DH), BF16),
            pltpu.VMEM(q.shape, BF16),
            pltpu.VMEM(cache.shape, BF16),
            pltpu.VMEM(fresh.shape, BF16),
            pltpu.SemaphoreType.DMA((2 + ROWS // OWN_TILE,)),
        ],
        out_shape=[
            jax.ShapeDtypeStruct((ROWS * GROUPS, DH), F32),
            jax.ShapeDtypeStruct((ROWS * GROUPS, 2 * DH), F32),
        ],
        compiler_params=params(50),
        cost_estimate=cost(keys),
        name="own_keys",
    )(meta, lengths, q, cache, fresh)


def prefix_call(name, plan, meta, pos, q, parts, state, rows=ROWS):
    n_parts = len(parts)
    keys = sum(p.shape[0] for p in parts)
    return pl.pallas_call(
        functools.partial(prefix_kernel, n_parts, plan),
        in_specs=[SMEM] + [VMEM] * (4 + n_parts),
        out_specs=[VMEM] * 2,
        scratch_shapes=[
            pltpu.VMEM((1 + ROWS // HALF, DH, keys), BF16),
            pltpu.VMEM((keys, 2 * DH), BF16),
        ],
        out_shape=[jax.ShapeDtypeStruct(s.shape, F32) for s in state],
        input_output_aliases={3 + n_parts: 0, 4 + n_parts: 1},
        compiler_params=params(20),
        cost_estimate=cost(keys, rows),
        name=name,
    )(meta, pos, q, *parts, *state)


def last_call(name, plan, places, meta, pos, q, parts, state, out_weight):
    n_parts = len(parts)
    keys = sum(p.shape[0] for p in parts)
    width = out_weight.shape[1]
    rows = TILE * len(places)
    terms = pl.pallas_call(
        functools.partial(last_kernel, n_parts, plan, places),
        in_specs=[SMEM] + [VMEM] * (5 + n_parts),
        out_specs=[VMEM] * len(places),
        scratch_shapes=[
            pltpu.VMEM((1 + ROWS // HALF, DH, keys), BF16),
            pltpu.VMEM((keys, 2 * DH), BF16),
            pltpu.VMEM((rows, GROUPS * DH), BF16),
        ],
        out_shape=[jax.ShapeDtypeStruct((TILE, width), BF16)] * len(places),
        compiler_params=params(20),
        cost_estimate=cost(keys, rows, 2 * rows * out_weight.size),
        name=name,
    )(meta, pos, q, *parts, *state, out_weight)
    return dict(zip(places, terms))


def on_device(queries, fresh_kv, positions, cache_kv, cache_lengths, out_weight):
    q = queries[0]
    own_kv = fresh_kv[0]
    section = lax.axis_index("section")
    seq = lax.axis_index("seq")
    head = lax.axis_index("head")

    meta = jnp.stack([section, seq >> 2, seq & 3, head >> 2, head & 3])
    pos = positions.reshape(-1, 1, HALF)
    lengths = cache_lengths.reshape(1, HALF)
    cache = cache_kv.reshape(ROWS // STEPS * CACHE, 2 * DH)

    other_kv = lax.ppermute(own_kv, "section", SWAP)
    mine = jnp.where(section == 0, own_kv[:HALF], other_kv[HALF:])
    blocks = [mine] + [lax.ppermute(mine, "seq", seq_perm(0, d)) for d in Z_ORDER[1:]]
    own_inputs = lax.optimization_barrier((mine, meta, lengths, pos))
    _, meta, lengths, pos = own_inputs
    state = own_call(meta, lengths, q, cache, own_kv)
    blocks[3], state = lax.optimization_barrier((blocks[3], state))
    near = jnp.concatenate(blocks, axis=0)
    far = {d: lax.ppermute(near, "seq", seq_perm(d, 0)) for d in (3, 1)}
    near_swapped = lax.ppermute(near, "section", SWAP)
    state = prefix_call("near_keys", NEAR, meta, pos, q, [near, near_swapped], state)
    sent, far[3], far[1], state = lax.optimization_barrier((near, far[3], far[1], state))
    far[2] = lax.ppermute(sent, "seq", seq_perm(2, 0))
    state = prefix_call("side_keys", SIDES, meta, pos, q, [far[3], far[1]], state, 1)
    far[3], far[1], state = lax.optimization_barrier((far[3], far[1], state))
    swapped = {d: lax.ppermute(far[d], "section", SWAP) for d in (3, 1)}
    far[2], state = lax.optimization_barrier((far[2], state))
    swapped[2] = lax.ppermute(far[2], "section", SWAP)
    rest = [swapped[3], swapped[1], far[2], swapped[2]]
    rest = (meta, pos, q, rest, state, out_weight)
    terms = last_call("last_keys_a", REST, PLACES_A, *rest)
    terms.update(last_call("last_keys_b", REST, PLACES_B, *rest))

    def move(term, dz, dx):
        return lax.ppermute(term, "head", head_perm(dz, dx))

    crossed = move(terms[1, 2], 1, 0)
    left_mirror = move(terms[1, 1], 0, 1)
    right_mirror = move(terms[1, 3], 0, 3)
    left = move(terms[0, 1], 0, 1)
    right = move(terms[0, 3], 0, 3)
    opposite = move(added(crossed, terms[0, 2]), 0, 2)
    mirror = move(added(left_mirror, right_mirror, terms[1, 0]), 1, 0)
    return added(terms[0, 0], mirror, opposite, left, right)[None]


def added(first, *others):
    total = first.astype(F32)
    for other in others:
        total = total + other.astype(F32)
    return total.astype(BF16)


def solution(mesh):
    in_specs = (
        P("section", "seq", "head"),
        P("section", "seq", "head"),
        P(),
        P("seq", None, "head"),
        P("seq"),
        P("head", None),
    )
    out_specs = P("section", ("seq", "head"), None)
    return jax.shard_map(
        on_device, mesh=mesh, in_specs=in_specs, out_specs=out_specs, check_vma=False
    )
```

```python
import functools
import math

import jax
import jax.numpy as jnp
from jax import lax
from jax.experimental import pallas as pl
from jax.experimental.pallas import tpu as pltpu
from jax.sharding import PartitionSpec as P

HQ = 64
KVH = 8
DH = 128
STEPS = 2
CACHE = 32
GROUPS = HQ // KVH
ROWS = 256
HALF = 128
TILE = 32
OWN_TILE = 16
LHS = TILE * GROUPS
NEG = -1e30
BIG = float(2**22)
EXP_SCALE = DH**-0.5 * math.log2(math.e)
BF16 = jnp.bfloat16
F32 = jnp.float32
Z_ORDER = (0, 2, 1, 3)


W_CHUNKS = 8
SLOTS = 8


def seq_perm(dy, dz):
    return [
        (y * 4 + z, ((y + dy) % 4) * 4 + (z + dz) % 4)
        for y in range(4)
        for z in range(4)
    ]


def head_perm(dz, dx):
    return [
        (z * 4 + x, (z ^ dz) * 4 + (x + dx) % 4)
        for z in range(2)
        for x in range(4)
    ]


SWAP = [(0, 1), (1, 0)]
NEAR = ((0, 0), (0, 1))
SIDES = ((3, 0), (1, 0))
REST = ((3, 1), (1, 1), (2, 0), (2, 1))
PLACES_A = ((1, 2), (1, 1), (1, 3), (0, 1), (0, 3))
PLACES_B = ((0, 2), (1, 0), (0, 0))


def stacked_queries(q_ref, first_row, first_col, tile=TILE):
    stack = jnp.concatenate(
        [q_ref[pl.ds(first_row, tile), g * DH : (g + 1) * DH] for g in range(GROUPS)],
        axis=0,
    )
    rows = lax.broadcasted_iota(jnp.int32, (tile * GROUPS, HALF), 0)
    cols = lax.broadcasted_iota(jnp.int32, (tile * GROUPS, HALF), 1)
    marks = jnp.where((rows & (tile - 1)) + first_col == cols, -BIG, 0.0).astype(BF16)
    return jnp.concatenate([stack, marks], axis=1)


def column_of(row, repeat=1, first=0):
    row = row.astype(F32)
    rows = lax.broadcasted_iota(jnp.int32, (HALF, HALF), 0) // repeat + first
    cols = lax.broadcasted_iota(jnp.int32, (HALF, HALF), 1)
    spread = jnp.where(rows == cols, jnp.broadcast_to(row, (HALF, HALF)), 0.0)
    return jnp.sum(spread, axis=1, keepdims=True)


def absorb(scores, old_max, values):
    width = scores.shape[1]
    top = scores[:, :DH]
    for j in range(DH, width, DH):
        top = jnp.maximum(top, scores[:, j : j + DH])
    new_max = jnp.max(top, axis=1, keepdims=True)
    if old_max is not None:
        new_max = jnp.maximum(old_max, new_max)
    else:
        new_max = jnp.broadcast_to(new_max, (scores.shape[0], DH))
    wide = jnp.concatenate([new_max] * (width // DH), axis=1)
    weights = jnp.exp2((scores - wide) * EXP_SCALE).astype(BF16)
    return new_max, jnp.dot(weights, values, preferred_element_type=F32)


def own_kernel(
    meta, len_ref, q_hbm, cache_hbm, fresh_hbm, m_out, a_out, kt, vs, q_ref, cache_ref, fresh_ref, sems
):
    keys = OWN_TILE // STEPS * CACHE
    tiles = ROWS // OWN_TILE

    @pl.when(meta[0] == 0)
    def _():
        m_out[...] = jnp.full(m_out.shape, NEG, F32)
        a_out[...] = jnp.zeros(a_out.shape, F32)

    @pl.when(meta[0] == 1)
    def _():
        def cache_copy(t):
            window = pl.ds(t * keys, keys)
            return pltpu.make_async_copy(
                cache_hbm.at[window], cache_ref.at[window], sems.at[2 + t]
            )

        fresh_copy = pltpu.make_async_copy(fresh_hbm, fresh_ref, sems.at[0])
        q_copy = pltpu.make_async_copy(q_hbm, q_ref, sems.at[1])
        fresh_copy.start()
        cache_copy(0).start()
        q_copy.start()
        for t in range(1, tiles):
            cache_copy(t).start()
        row = lax.broadcasted_iota(jnp.int32, (OWN_TILE, keys), 0)
        key = lax.broadcasted_iota(jnp.int32, (OWN_TILE, keys), 1)
        same = (key // CACHE) == (row // STEPS)
        nth = (key % CACHE).astype(F32)
        frow = lax.broadcasted_iota(jnp.int32, (OWN_TILE, HALF), 0)
        fkey = lax.broadcasted_iota(jnp.int32, (OWN_TILE, HALF), 1)
        for slot in range(SLOTS):
            kt[slot, DH + OWN_TILE :, :] = jnp.zeros((DH - OWN_TILE, keys + HALF), BF16)
            vs[slot, :, DH:] = jnp.ones((keys + HALF, DH), BF16)
        fresh_copy.wait()
        for t in range(tiles):
            slot = t % SLOTS
            block, mine = t * OWN_TILE // HALF, frow + t * OWN_TILE % HALF
            if t * OWN_TILE % HALF == 0:
                lengths = column_of(len_ref[...], STEPS, block * (HALF // STEPS))
                fresh = slice(block * HALF, (block + 1) * HALF)
                for at in range(SLOTS):
                    kt[at, :DH, keys:] = fresh_ref[fresh, :DH].T
                    vs[at, keys:, :DH] = fresh_ref[fresh, DH:]
            if t == 0:
                q_copy.wait()
            if t % SLOTS == 0:
                for ahead in range(t, t + SLOTS):
                    cache_copy(ahead).wait()
            kt[slot, :DH, :keys] = cache_ref[t * keys : (t + 1) * keys, :DH].T
            first = t * OWN_TILE % HALF
            seen = same & (nth < lengths[first : first + OWN_TILE])
            kt[slot, DH : DH + OWN_TILE, :keys] = jnp.where(seen, 0.0, 1.0).astype(BF16)
            seen = ((mine // STEPS) == (fkey // STEPS)) & (fkey <= mine)
            kt[slot, DH : DH + OWN_TILE, keys:] = jnp.where(seen, 0.0, 1.0).astype(BF16)
            vs[slot, :keys, :DH] = cache_ref[t * keys : (t + 1) * keys, DH:]
            lhs = stacked_queries(q_ref, t * OWN_TILE, 0, OWN_TILE)
            scores = jnp.dot(lhs, kt[slot], preferred_element_type=F32)
            new_max, total = absorb(scores, None, vs[slot])
            start = t * OWN_TILE // TILE * LHS + t * OWN_TILE % TILE
            for g in range(GROUPS):
                rows = slice(start + g * TILE, start + g * TILE + OWN_TILE)
                m_out[rows, :] = new_max[g * OWN_TILE : (g + 1) * OWN_TILE]
                a_out[rows, :] = total[g * OWN_TILE : (g + 1) * OWN_TILE]


def load_keys(parts, kt, vs):
    count = parts[0].shape[0]
    for i, part in enumerate(parts):
        kt[0, :, i * count : (i + 1) * count] = part[:, :DH].T
        vs[i * count : (i + 1) * count, :DH] = part[:, DH:]
    vs[:, DH:] = jnp.ones((len(parts) * count, DH), BF16)


def load_mask(meta, plan, block, pos_ref, kt):
    own = (meta[1] * 4 + meta[2]) * 2
    bound = jnp.where(meta[0] == 1, 1e9, column_of(pos_ref[own + block]))
    pieces = [(dy, dz, flip) for dy, flip in plan for dz in Z_ORDER]
    for j, (dy, dz, flip) in enumerate(pieces):
        source = ((meta[1] - dy) & 3) * 4 + ((meta[2] - dz) & 3)
        key_pos = pos_ref[source * 2 + (meta[0] ^ flip)].astype(F32)
        hidden = jnp.where(key_pos > bound, 1.0, 0.0).astype(BF16)
        kt[1 + block, :, j * HALF : (j + 1) * HALF] = hidden


def prefix_kernel(n_parts, plan, meta, pos_ref, q_ref, *refs):
    parts = refs[:n_parts]
    m_in, a_in, m_out, a_out, kt, vs = refs[n_parts:]
    load_keys(parts, kt, vs)
    for block in range(ROWS // HALF):
        load_mask(meta, plan, block, pos_ref, kt)
    tiles = ROWS // TILE

    def scores_of(t):
        return scores_at(q_ref, kt, t * TILE, t * TILE % HALF, t * TILE // HALF)

    ready = scores_of(0)
    for t in range(tiles):
        following = scores_of(t + 1) if t + 1 < tiles else None
        rows = slice(t * LHS, (t + 1) * LHS)
        new_max, total = fold_in(ready, m_in[rows, :], a_in[rows, :], vs)
        m_out[rows, :] = new_max
        a_out[rows, :] = total
        ready = following


def scores_at(q_ref, kt, first_row, first_col, block):
    lhs = stacked_queries(q_ref, first_row, first_col)
    keys = jnp.concatenate([kt[0], kt[1 + block]], axis=0)
    return jnp.dot(lhs, keys, preferred_element_type=F32)


def fold_in(scores, old_max, old_total, vs):
    new_max, total = absorb(scores, old_max, vs[...])
    factor = jnp.exp2((old_max - new_max) * EXP_SCALE)
    return new_max, old_total * jnp.concatenate([factor, factor], axis=1) + total


def last_kernel(n_parts, plan, places, meta, pos_ref, q_ref, *refs):
    parts = refs[:n_parts]
    m_in, a_in, w_ref = refs[n_parts : n_parts + 3]
    outs = refs[n_parts + 3 : n_parts + 3 + len(places)]
    kt, vs, att = refs[n_parts + 3 + len(places) :]
    cols = w_ref.shape[1] // W_CHUNKS
    load_keys(parts, kt, vs)
    for block in range(ROWS // HALF):
        load_mask(meta, plan, block, pos_ref, kt)
    tiles = HALF // TILE

    def place_of(t):
        dz, dx = places[t]
        return meta[3] ^ dz, (meta[4] + dx) & (tiles - 1)

    def scores_of(t):
        block, tile = place_of(t)
        first_col = pl.multiple_of(tile * TILE, TILE)
        first_row = pl.multiple_of(block * HALF + first_col, TILE)
        return scores_at(q_ref, kt, first_row, first_col, block)

    ready = scores_of(0)
    for t in range(len(places)):
        following = scores_of(t + 1) if t + 1 < len(places) else None
        block, tile = place_of(t)
        rows = pl.ds(pl.multiple_of((block * tiles + tile) * LHS, LHS), LHS)
        _, total = fold_in(ready, m_in[rows, :], a_in[rows, :], vs)
        attended = (total[:, :DH] / total[:, DH:]).astype(BF16)
        for g in range(GROUPS):
            att[t * TILE : (t + 1) * TILE, g * DH : (g + 1) * DH] = attended[
                g * TILE : (g + 1) * TILE
            ]
        ready = following
    for c in range(W_CHUNKS):
        window = slice(c * cols, (c + 1) * cols)
        term = jnp.dot(att[...], w_ref[:, window], preferred_element_type=F32)
        term = term.astype(BF16)
        for t in range(len(places)):
            outs[t][:, window] = term[t * TILE : (t + 1) * TILE]


def params(mebibytes):
    return pltpu.CompilerParams(vmem_limit_bytes=mebibytes * 2**20)


def cost(keys, rows=ROWS, extra=0):
    work = rows * GROUPS * keys
    return pl.CostEstimate(
        flops=8 * DH * work + extra, bytes_accessed=rows * 2**14, transcendentals=work
    )


VMEM = pl.BlockSpec(memory_space=pltpu.VMEM)
SMEM = pl.BlockSpec(memory_space=pltpu.SMEM)
HBM = pl.BlockSpec(memory_space=pltpu.HBM)


def own_call(meta, lengths, q, cache, fresh):
    keys = OWN_TILE // STEPS * CACHE + HALF
    return pl.pallas_call(
        own_kernel,
        in_specs=[SMEM, VMEM, HBM, HBM, HBM],
        out_specs=[VMEM] * 2,
        scratch_shapes=[
            pltpu.VMEM((SLOTS, 2 * DH, keys), BF16),
            pltpu.VMEM((SLOTS, keys, 2 * DH), BF16),
            pltpu.VMEM(q.shape, BF16),
            pltpu.VMEM(cache.shape, BF16),
            pltpu.VMEM(fresh.shape, BF16),
            pltpu.SemaphoreType.DMA((2 + ROWS // OWN_TILE,)),
        ],
        out_shape=[
            jax.ShapeDtypeStruct((ROWS * GROUPS, DH), F32),
            jax.ShapeDtypeStruct((ROWS * GROUPS, 2 * DH), F32),
        ],
        compiler_params=params(50),
        cost_estimate=cost(keys),
        name="own_keys",
    )(meta, lengths, q, cache, fresh)


def prefix_call(name, plan, meta, pos, q, parts, state, rows=ROWS):
    n_parts = len(parts)
    keys = sum(p.shape[0] for p in parts)
    return pl.pallas_call(
        functools.partial(prefix_kernel, n_parts, plan),
        in_specs=[SMEM] + [VMEM] * (4 + n_parts),
        out_specs=[VMEM] * 2,
        scratch_shapes=[
            pltpu.VMEM((1 + ROWS // HALF, DH, keys), BF16),
            pltpu.VMEM((keys, 2 * DH), BF16),
        ],
        out_shape=[jax.ShapeDtypeStruct(s.shape, F32) for s in state],
        input_output_aliases={3 + n_parts: 0, 4 + n_parts: 1},
        compiler_params=params(20),
        cost_estimate=cost(keys, rows),
        name=name,
    )(meta, pos, q, *parts, *state)


def last_call(name, plan, places, meta, pos, q, parts, state, out_weight):
    n_parts = len(parts)
    keys = sum(p.shape[0] for p in parts)
    width = out_weight.shape[1]
    rows = TILE * len(places)
    terms = pl.pallas_call(
        functools.partial(last_kernel, n_parts, plan, places),
        in_specs=[SMEM] + [VMEM] * (5 + n_parts),
        out_specs=[VMEM] * len(places),
        scratch_shapes=[
            pltpu.VMEM((1 + ROWS // HALF, DH, keys), BF16),
            pltpu.VMEM((keys, 2 * DH), BF16),
            pltpu.VMEM((rows, GROUPS * DH), BF16),
        ],
        out_shape=[jax.ShapeDtypeStruct((TILE, width), BF16)] * len(places),
        compiler_params=params(20),
        cost_estimate=cost(keys, rows, 2 * rows * out_weight.size),
        name=name,
    )(meta, pos, q, *parts, *state, out_weight)
    return dict(zip(places, terms))


def on_device(queries, fresh_kv, positions, cache_kv, cache_lengths, out_weight):
    q = queries[0]
    own_kv = fresh_kv[0]
    section = lax.axis_index("section")
    seq = lax.axis_index("seq")
    head = lax.axis_index("head")

    meta = jnp.stack([section, seq >> 2, seq & 3, head >> 2, head & 3])
    pos = positions.reshape(-1, 1, HALF)
    lengths = cache_lengths.reshape(1, HALF)
    cache = cache_kv.reshape(ROWS // STEPS * CACHE, 2 * DH)

    other_kv = lax.ppermute(own_kv, "section", SWAP)
    mine = jnp.where(section == 0, own_kv[:HALF], other_kv[HALF:])
    blocks = [mine] + [lax.ppermute(mine, "seq", seq_perm(0, d)) for d in Z_ORDER[1:]]
    own_inputs = lax.optimization_barrier((mine, meta, lengths, pos))
    _, meta, lengths, pos = own_inputs
    state = own_call(meta, lengths, q, cache, own_kv)
    blocks[3], state = lax.optimization_barrier((blocks[3], state))
    near = jnp.concatenate(blocks, axis=0)
    far = {d: lax.ppermute(near, "seq", seq_perm(d, 0)) for d in (3, 1)}
    near_swapped = lax.ppermute(near, "section", SWAP)
    state = prefix_call("near_keys", NEAR, meta, pos, q, [near, near_swapped], state)
    sent, far[3], far[1], state = lax.optimization_barrier((near, far[3], far[1], state))
    far[2] = lax.ppermute(sent, "seq", seq_perm(2, 0))
    state = prefix_call("side_keys", SIDES, meta, pos, q, [far[3], far[1]], state, 1)
    far[3], far[1], state = lax.optimization_barrier((far[3], far[1], state))
    swapped = {d: lax.ppermute(far[d], "section", SWAP) for d in (3, 1)}
    far[2], state = lax.optimization_barrier((far[2], state))
    swapped[2] = lax.ppermute(far[2], "section", SWAP)
    rest = [swapped[3], swapped[1], far[2], swapped[2]]
    rest = (meta, pos, q, rest, state, out_weight)
    terms = last_call("last_keys_a", REST, PLACES_A, *rest)
    terms.update(last_call("last_keys_b", REST, PLACES_B, *rest))

    def move(term, dz, dx):
        return lax.ppermute(term, "head", head_perm(dz, dx))

    crossed = move(terms[1, 2], 1, 0)
    left_mirror = move(terms[1, 1], 0, 1)
    right_mirror = move(terms[1, 3], 0, 3)
    left = move(terms[0, 1], 0, 1)
    right = move(terms[0, 3], 0, 3)
    opposite = move(added(crossed, terms[0, 2]), 0, 2)
    mirror = move(added(left_mirror, right_mirror, terms[1, 0]), 1, 0)
    return added(terms[0, 0], mirror, opposite, right, left)[None]


def added(first, *others):
    total = first.astype(F32)
    for other in others:
        total = total + other.astype(F32)
    return total.astype(BF16)


def solution(mesh):
    in_specs = (
        P("section", "seq", "head"),
        P("section", "seq", "head"),
        P(),
        P("seq", None, "head"),
        P("seq"),
        P("head", None),
    )
    out_specs = P("section", ("seq", "head"), None)
    return jax.shard_map(
        on_device, mesh=mesh, in_specs=in_specs, out_specs=out_specs, check_vma=False
    )
```
